512 devices in a mesh: src: 32 (over x, y, z_hi), tgt: 16 (over z_lo, core).
Axes of the slice: x: 4, y: 4, z: 16 (z_hi: 2, z_lo: 8; z = z_hi * 8 + z_lo), core: 2. Of those that a mesh axis runs over, the one named last changes fastest.
Arguments:
- points_src: float32 [32768, 128], P(('src', 'tgt')), may hold values from -7 to 7
- points_tgt: float32 [8192, 128], P('tgt'), may hold values from -2 to 2
- log_source: float32 [32768], P(('src', 'tgt')), may hold values from -3 to 5.2
- log_target: float32 [8192], P('tgt'), may hold values from -3 to 3
- target_potential: float32 [8192], P('tgt'), may hold values from -4 to 60
Outputs:
- source_potential: float32 [32768], P(('src', 'tgt'))
- target_new: float32 [8192], P('tgt')
- mapped: float32 [32768, 128], P(('src', 'tgt'))
The draws below stay inside these ranges and needn't reach their ends.
All inputs are finite; a program needn't handle non-finite values.
Results may differ from the reference program's by a relative error of at most 0.0003.
Values sent between devices are 32-bit elements; how exact they have to be, the bound alone decides.
A program may use at most 64 MiB of HBM per device.

```python
import jax
import jax.numpy as jnp
from jax import lax

DIM = 128
NS = 32768
NT = 8192


def corner_signs(key):
    flips = jax.random.bernoulli(jax.random.fold_in(key, 5), 0.5, (DIM,))
    return jnp.where(flips, 2.0, -2.0).astype(jnp.float32)


def draw_points_src(key, part):
    signs = corner_signs(key)
    key = jax.random.fold_in(key, 11)
    noise_key = jax.random.fold_in(key, 0)
    values = jax.random.normal(noise_key, (NS, DIM), jnp.float32) * 0.2
    result = jnp.clip(values, -1.2, 1.2)
    return result.at[NS // 2 + 1].set(signs)


def draw_points_tgt(key, part):
    signs = corner_signs(key)
    key = jax.random.fold_in(key, 13)
    values = jnp.clip(jax.random.normal(key, (NT, DIM), jnp.float32) * 0.2, -1.2, 1.2)
    return values.at[2].set(signs).at[NT - 3].set(-signs)


def draw_log_source(key, part):
    key = jax.random.fold_in(key, 23)
    ramp = jnp.arange(NS).astype(jnp.float32) / float(max(NS - 1, 1))
    return jnp.clip(jax.random.normal(key, (NS,), jnp.float32), -3.0, 3.0) + 1.1 * ramp


def draw_target_potential(key, part):
    key = jax.random.fold_in(key, 37)
    values = jnp.clip(jax.random.normal(key, (NT,), jnp.float32), -4.0, 4.0)
    return values.at[NT - 3].set(-4.0)


def levels(rng, dims, cuts, low, largest):
    gain = 1.0
    for position, shards_of in cuts:
        draws = jax.random.uniform(jax.random.fold_in(jax.random.fold_in(rng, 6), position), (shards_of,), jnp.float32, low / len(cuts), largest / len(cuts))
        gain = gain * jnp.repeat(jnp.exp(draws), dims[position] // shards_of).reshape((-1,) + (1,) * (len(dims) - 1 - position))
    return gain


def noise(rng, dims, scale, most, cuts=(), kind=jnp.bfloat16):
    gain = levels(rng, dims, cuts, -0.22, 0.18) if cuts else 1.0
    entries = jax.random.normal(rng, dims, jnp.float32) * scale * gain
    return jnp.minimum(jnp.maximum(entries, -most), most).astype(kind)


def setup_inputs(seed: int = 0) -> dict:
    splits = jax.random.split(jax.random.key(seed), 6)
    points_src = draw_points_src(jax.random.fold_in(splits[5], 71), 0)
    points_tgt = draw_points_tgt(jax.random.fold_in(splits[5], 71), 0)
    log_source = draw_log_source(jax.random.fold_in(splits[5], 71), 0)
    log_target = noise(splits[3], (NT,), 1.0, 3.0, ((0, 16),), jnp.float32)
    target_potential = draw_target_potential(jax.random.fold_in(splits[5], 71), 0)
    return {"points_src": points_src, "points_tgt": points_tgt, "log_source": log_source, "log_target": log_target, "target_potential": target_potential}


epsilon = 0.5


def pair_cost(rows_a, rows_b):
    cross = jnp.dot(rows_a, rows_b.T, precision=lax.Precision.HIGHEST, preferred_element_type=jnp.float32)
    left = 0.5 * jnp.sum(rows_a * rows_a, axis=1)
    right = 0.5 * jnp.sum(rows_b * rows_b, axis=1)
    return left[:, None] + right[None, :] - cross


def reference(points_src, points_tgt, log_source, log_target, target_potential):
    row_block = min(512, NS)
    col_block = min(256, NT)
    src_groups = points_src.reshape(NS // row_block, row_block, DIM)
    mass_groups = log_source.reshape(NS // row_block, row_block)

    def source_step(inputs):
        rows, masses = inputs
        scores = (target_potential[None, :] - pair_cost(rows, points_tgt)) / epsilon
        peak = jnp.max(scores, axis=1)
        total = jnp.sum(jnp.exp(scores - peak[:, None]), axis=1)
        return epsilon * (masses - peak - jnp.log(total))

    source_potential = lax.map(source_step, (src_groups, mass_groups)).reshape(NS)

    tgt_groups = points_tgt.reshape(NT // col_block, col_block, DIM)
    tmass_groups = log_target.reshape(NT // col_block, col_block)

    def target_step(inputs):
        cols, masses = inputs
        scores = (source_potential[:, None] - pair_cost(points_src, cols)) / epsilon
        peak = jnp.max(scores, axis=0)
        total = jnp.sum(jnp.exp(scores - peak[None, :]), axis=0)
        return epsilon * (masses - peak - jnp.log(total))

    target_new = lax.map(target_step, (tgt_groups, tmass_groups)).reshape(NT)

    def map_step(rows):
        scores = (target_new[None, :] - pair_cost(rows, points_tgt)) / epsilon
        peak = jnp.max(scores, axis=1)
        weights = jnp.exp(scores - peak[:, None])
        total = jnp.sum(weights, axis=1)
        summed = jnp.dot(weights, points_tgt, precision=lax.Precision.HIGHEST, preferred_element_type=jnp.float32)
        return summed / total[:, None]

    mapped = lax.map(map_step, src_groups).reshape(NS, DIM)
    return source_potential, target_new, mapped
```

```python
import jax
import jax.numpy as jnp
from jax import lax
from jax.experimental import pallas as pl
from jax.experimental.pallas import tpu as pltpu
from jax.sharding import PartitionSpec as P

MESH = pl.DeviceIdType.MESH
F32 = jnp.float32
BF16 = jnp.bfloat16
ROWS = 64
SLICE = 32
PLANE = 16
NEAR = (3, -3, 2, -2, 1, -1)


def lse0(values):
    peak = jnp.max(values, axis=0, keepdims=True)
    return peak + jnp.log(jnp.sum(jnp.exp(values - peak), axis=0, keepdims=True))


def kernel(
    ps, pt, ls, lt, gp,
    out_f, out_t, out_m,
    xs, tb, y2, yt, aa, ltb, sc, rb, uu, lsum, cl, cb, vv, mp, tn, mm, mb, wt,
    xs_s, xs_r, tb_s, tb_r, rb_s, rb_r, cb_s, cb_r, tn_s, tn_r, mb_s, mb_r,
):
    s = lax.axis_index("src")
    t = lax.axis_index("tgt")
    q = s // 2
    zh = s % 2
    zl = t // 2
    c = t % 2
    z = zh * 8 + zl
    x = q // 4
    y = q % 4
    me = z * 2 + c

    def plane_index(k):
        return ((x + k // 4) % 4) * 4 + (y + k % 4) % 4

    def plane_device(p):
        return (p * 2 + zh, t)

    def column_device(to_z, to_c):
        return (q * 2 + to_z // 8, (to_z % 8) * 2 + to_c)

    def plane_copy(src, dst, send, recv, p, slot):
        return pltpu.make_async_remote_copy(
            src_ref=src, dst_ref=dst, send_sem=send.at[p], recv_sem=recv.at[slot],
            device_id=plane_device(p), device_id_type=MESH,
        )

    def column_copy(buf, slot, send, recv, k, to_z, to_c):
        return pltpu.make_async_remote_copy(
            src_ref=buf.at[slot], dst_ref=buf.at[slot], send_sem=send.at[k], recv_sem=recv.at[slot],
            device_id=column_device(to_z, to_c), device_id_type=MESH,
        )

    barrier = pltpu.get_barrier_semaphore()

    def greet_column(k, carry):
        pl.semaphore_signal(
            barrier, inc=1, device_id=column_device((z + k // 2) % 16, (c + k % 2) % 2), device_id_type=MESH
        )
        return carry

    def greet_plane(k, carry):
        pl.semaphore_signal(barrier, inc=1, device_id=plane_device(plane_index(k)), device_id_type=MESH)
        return carry

    lax.fori_loop(1, 32, greet_column, 0)
    lax.fori_loop(1, PLANE, greet_plane, 0)

    xs[pl.ds(q, 1)] = ps[...][None]
    tb[pl.ds(t, 1), 0:SLICE] = pt[pl.ds(q * SLICE, SLICE), :][None]
    tb[pl.ds(t, 1), SLICE : SLICE + 1] = gp[pl.ds(q // 4, 1), :][None]
    tb[pl.ds(t, 1), SLICE + 1 : SLICE + 2] = lt[pl.ds(q // 4, 1), :][None]

    pl.semaphore_wait(barrier, 31 + 15)

    far = 4 - 8 * c
    target_sends = []
    for d in (far,) + NEAR:
        for to_c in range(2):
            target_sends.append(column_copy(tb, t, tb_s, tb_r, len(target_sends), (z + d + 16) % 16, to_c))
    target_sends.append(column_copy(tb, t, tb_s, tb_r, len(target_sends), z, 1 - c))
    for copy in target_sends:
        copy.start()

    def send_points(k, carry):
        p = plane_index(16 - k)
        plane_copy(xs.at[q], xs.at[q], xs_s, xs_r, p, q).start()
        return carry

    lax.fori_loop(1, PLANE, send_points, 0)

    sq = jnp.concatenate([ps[...] * ps[...], jnp.zeros((128 - ROWS, 128), F32)], axis=0)
    norm = jnp.sum(sq.T, axis=0, keepdims=True)

    lane = lax.broadcasted_iota(jnp.int32, (SLICE, 128), 1)
    sub = lax.broadcasted_iota(jnp.int32, (SLICE, 128), 0)
    mine = lane == sub + (q % 4) * SLICE

    def take_targets(k, carry):
        e = k // 2
        half = (e + 1) // 2
        off = (e % 2) * half + (1 - e % 2) * ((8 - half) % 8)
        slot = ((zl + off) % 8) * 2 + k % 2

        @pl.when(slot != t)
        def _():
            column_copy(tb, slot, tb_s, tb_r, 0, z, 1 - c).wait_recv()

        pts = tb[pl.ds(slot, 1), 0:SLICE][0]
        grow = tb[pl.ds(slot, 1), SLICE : SLICE + 1][0]
        lrow = tb[pl.ds(slot, 1), SLICE + 1 : SLICE + 2][0]
        rows = pl.ds(pl.multiple_of(slot * SLICE, SLICE), SLICE)
        a = jnp.sum(jnp.where(mine, 2.0 * grow, 0.0) - pts * pts, axis=1, keepdims=True)
        l = jnp.sum(jnp.where(mine, lrow, 0.0), axis=1, keepdims=True)
        aa[rows, :] = jnp.broadcast_to(a, (SLICE, 128))
        ltb[rows, :] = jnp.broadcast_to(l, (SLICE, 128))
        y2[rows, :] = 2.0 * pts
        return carry

    lax.fori_loop(0, 16, take_targets, 0)
    for b in range(4):
        yb = 0.5 * y2[b * 128 : (b + 1) * 128, :].T
        hi = yb.astype(BF16)
        yt[0:128, b * 128 : (b + 1) * 128] = hi
        yt[128:256, b * 128 : (b + 1) * 128] = (yb - hi.astype(F32)).astype(BF16)

    def pair_at(m, b):
        a = m + (m // 2) * (5 - 2 * m)
        return ((x + a) % 4) * 2 + (y // 2 + b) % 2

    def take_sources(k, carry):
        pair = pair_at(k // 2, k % 2)
        for h in range(2):
            p = 2 * pair + h

            @pl.when(p != q)
            def _():
                plane_copy(xs.at[p], xs.at[p], xs_s, xs_r, p, p).wait_recv()

        pts = xs[pl.ds(2 * pair, 2)].reshape(128, 128)
        prod = lax.dot_general(
            y2[...], pts, (((1,), (1,)), ((), ())),
            precision=lax.Precision.HIGHEST, preferred_element_type=F32,
        )
        score = prod + aa[...]
        sc[pl.ds(pair, 1)] = score[None]
        rb[pl.ds(q, 1), pl.ds(pair, 1)] = lse0(score)[None]
        return carry

    lax.fori_loop(0, 8, take_sources, 0)
    half = lax.broadcasted_iota(jnp.int32, (1, 128), 1) // 64 == q % 2
    both = jnp.concatenate([ls[...], ls[...]], axis=1)
    rb[pl.ds(q, 1), 8:9] = jnp.where(half, both, 0.0)[None]

    def send_rows(k, carry):
        p = plane_index(16 - k)
        plane_copy(rb.at[q], rb.at[q], rb_s, rb_r, p, q).start()
        return carry

    lax.fori_loop(1, PLANE, send_rows, 0)

    def wait_rows(k, carry):
        p = plane_index(k)
        plane_copy(rb.at[p], rb.at[p], rb_s, rb_r, p, p).wait_recv()
        return carry

    lax.fori_loop(1, PLANE, wait_rows, 0)
    part = rb[:, 0:8]
    rowlse = lse0(part)[0]
    uu[...] = rowlse
    for b in range(8):
        lsum[b : b + 1, :] = rb[2 * b, 8:9] + rb[2 * b + 1, 8:9]

    own_lse = uu[pl.ds(q // 2, 1), :]
    own_lse = jnp.where(q % 2 == 0, own_lse, pltpu.roll(own_lse, 64, 1))
    out_f[...] = 0.5 * (ls[...] + norm[:, 0:ROWS] - own_lse[:, 0:ROWS])
    u = lsum[...] - rowlse

    def columns(j, carry):
        rows = pl.ds(pl.multiple_of(j * 32, 32), 32)
        vals = [u[b : b + 1, :] + sc[b, rows, :] for b in range(8)]
        peak = vals[0]
        for v in vals[1:]:
            peak = jnp.maximum(peak, v)
        total = jnp.exp(vals[0] - peak)
        for v in vals[1:]:
            total = total + jnp.exp(v - peak)
        cl[rows, :] = peak + jnp.log(total)
        return carry

    lax.fori_loop(0, 16, columns, 0)
    for b in range(4):
        cb[pl.ds(me, 1), b : b + 1] = lse0(cl[b * 128 : (b + 1) * 128, :].T)[None]

    def send_columns(k, carry):
        m = k // 2
        near = (m + 1) // 2
        d = (8 - near) * (1 - m % 2) + (8 + near) * (m % 2)
        column_copy(cb, me, cb_s, cb_r, k, (z + d) % 16, k % 2).start()
        return carry

    lax.fori_loop(0, 30, send_columns, 0)
    column_copy(cb, me, cb_s, cb_r, 30, z, 1 - c).start()

    def wait_columns(k, carry):
        slot = (me + k) % 32
        column_copy(cb, slot, cb_s, cb_r, 0, z, 1 - c).wait_recv()
        return carry

    lax.fori_loop(1, 32, wait_columns, 0)
    collse = lse0(cb[...])[0]
    for b in range(4):
        mp[b] = collse[b : b + 1, :]
        spread = jnp.broadcast_to(collse[b : b + 1, :], (128, 128)).T
        vv[b * 128 : (b + 1) * 128, :] = ltb[b * 128 : (b + 1) * 128, :] - spread
    tn[pl.ds(q, 1)] = mp[pl.ds(t // 4, 1)]

    def send_new(k, carry):
        p = plane_index(16 - k)
        plane_copy(tn.at[q], tn.at[q], tn_s, tn_r, p, q).start()
        return carry

    lax.fori_loop(1, PLANE, send_new, 0)

    def map_pair(k, carry):
        pair = pair_at(3 - k // 2, 1 - k % 2)
        val = vv[...] + sc[pl.ds(pair, 1)][0]
        peak = jnp.max(val, axis=0, keepdims=True)
        w = jnp.exp(val - peak)
        total = jnp.sum(w, axis=0, keepdims=True)
        hi = w.astype(BF16)
        lo = (w - hi.astype(F32)).astype(BF16)
        first = jnp.dot(yt[...], hi, preferred_element_type=F32)
        second = jnp.dot(yt[0:128, :], lo, preferred_element_type=F32)
        n = (first[0:128] + first[128:256] + second).T
        for h in range(2):
            p = 2 * pair + h
            mm[pl.ds(p, 1), 0:ROWS] = n[h * ROWS : (h + 1) * ROWS][None]
            mm[pl.ds(p, 1), ROWS : ROWS + 1] = peak[None]
            mm[pl.ds(p, 1), ROWS + 1 : ROWS + 2] = total[None]

            @pl.when(p != q)
            def _():
                plane_copy(mm.at[p], mb.at[q], mb_s, mb_r, p, q).start()

        return carry

    lax.fori_loop(0, 8, map_pair, 0)
    mb[pl.ds(q, 1)] = mm[pl.ds(q, 1)]

    def wait_new(k, carry):
        p = plane_index(k)
        plane_copy(tn.at[p], tn.at[p], tn_s, tn_r, p, p).wait_recv()
        return carry

    lax.fori_loop(1, PLANE, wait_new, 0)
    pieces = tn[...].reshape(16, 128)
    lane16 = lax.broadcasted_iota(jnp.int32, (16, 128), 1) // SLICE
    sub16 = lax.broadcasted_iota(jnp.int32, (16, 128), 0) % 4
    whole = jnp.zeros((16, 128), F32)
    for k in range(4):
        turned = pltpu.roll(pieces, ((k - t % 4 + 4) % 4) * SLICE, 1)
        whole = whole + jnp.where((lane16 == k) & (sub16 == k), turned, 0.0)
    for b in range(4):
        row = jnp.sum(whole[4 * b : 4 * b + 4], axis=0, keepdims=True)
        out_t[b : b + 1, :] = gp[b : b + 1, :] + 0.5 * (lt[b : b + 1, :] - row)

    def wait_map(k, carry):
        p = plane_index(k)
        plane_copy(mm.at[p], mb.at[p], mb_s, mb_r, p, p).wait_recv()
        return carry

    lax.fori_loop(1, PLANE, wait_map, 0)
    peaks = jnp.concatenate([mb[p, ROWS : ROWS + 1] for p in range(16)], axis=0)
    totals = jnp.concatenate([mb[p, ROWS + 1 : ROWS + 2] for p in range(16)], axis=0)
    scale = jnp.exp(peaks - jnp.max(peaks, axis=0, keepdims=True))
    scale = scale / jnp.sum(scale * totals, axis=0, keepdims=True)
    wt[...] = jnp.concatenate([scale, jnp.zeros((112, 128), F32)], axis=0).T
    weights = wt[pl.ds(pl.multiple_of((q % 2) * ROWS, ROWS), ROWS), :]
    total = weights[:, 0:1] * mb[0, 0:ROWS]
    for p in range(1, 16):
        total = total + weights[:, p : p + 1] * mb[p, 0:ROWS]
    out_m[...] = total

    for copy in target_sends:
        copy.wait_send()

    def sent_plane(k, carry):
        p = plane_index(k)
        plane_copy(xs.at[q], xs.at[q], xs_s, xs_r, p, q).wait_send()
        plane_copy(rb.at[q], rb.at[q], rb_s, rb_r, p, q).wait_send()
        plane_copy(tn.at[q], tn.at[q], tn_s, tn_r, p, q).wait_send()
        plane_copy(mm.at[p], mb.at[q], mb_s, mb_r, p, q).wait_send()
        return carry

    lax.fori_loop(1, PLANE, sent_plane, 0)

    def sent_columns(k, carry):
        column_copy(cb, me, cb_s, cb_r, k, z, 1 - c).wait_send()
        return carry

    lax.fori_loop(0, 31, sent_columns, 0)


def shards(points_src, points_tgt, log_source, log_target, target_potential):
    vmem = pl.BlockSpec(memory_space=pltpu.VMEM)
    dma = pltpu.SemaphoreType.DMA
    source_potential, target_new, mapped = pl.pallas_call(
        kernel,
        name="sinkhorn",
        out_shape=(
            jax.ShapeDtypeStruct((1, ROWS), F32),
            jax.ShapeDtypeStruct((4, 128), F32),
            jax.ShapeDtypeStruct((ROWS, 128), F32),
        ),
        in_specs=[vmem] * 5,
        out_specs=(vmem,) * 3,
        scratch_shapes=[
            pltpu.VMEM((16, ROWS, 128), F32),
            pltpu.VMEM((16, 40, 128), F32),
            pltpu.VMEM((512, 128), F32),
            pltpu.VMEM((256, 512), BF16),
            pltpu.VMEM((512, 128), F32),
            pltpu.VMEM((512, 128), F32),
            pltpu.VMEM((8, 512, 128), F32),
            pltpu.VMEM((16, 16, 128), F32),
            pltpu.VMEM((8, 128), F32),
            pltpu.VMEM((8, 128), F32),
            pltpu.VMEM((512, 128), F32),
            pltpu.VMEM((32, 4, 128), F32),
            pltpu.VMEM((512, 128), F32),
            pltpu.VMEM((4, 1, 128), F32),
            pltpu.VMEM((16, 1, 128), F32),
            pltpu.VMEM((16, 72, 128), F32),
            pltpu.VMEM((16, 72, 128), F32),
            pltpu.VMEM((128, 128), F32),
            dma((16,)), dma((16,)),
            dma((16,)), dma((16,)),
            dma((16,)), dma((16,)),
            dma((32,)), dma((32,)),
            dma((16,)), dma((16,)),
            dma((16,)), dma((16,)),
        ],
        compiler_params=pltpu.CompilerParams(
            collective_id=0, has_side_effects=True, vmem_limit_bytes=40 * 2**20
        ),
    )(
        points_src,
        points_tgt,
        log_source.reshape(1, ROWS),
        log_target.reshape(4, 128),
        target_potential.reshape(4, 128),
    )
    return source_potential.reshape(ROWS), target_new.reshape(512), mapped


def solution(mesh):
    return jax.shard_map(
        shards,
        mesh=mesh,
        in_specs=(P(("src", "tgt"), None), P("tgt", None), P(("src", "tgt")), P("tgt"), P("tgt")),
        out_specs=(P(("src", "tgt")), P("tgt"), P(("src", "tgt"), None)),
        check_vma=False,
    )
```

```python
import jax
import jax.numpy as jnp
from jax import lax
from jax.experimental import pallas as pl
from jax.experimental.pallas import tpu as pltpu
from jax.sharding import PartitionSpec as P

MESH = pl.DeviceIdType.MESH
F32 = jnp.float32
BF16 = jnp.bfloat16
ROWS = 64
SLICE = 32
QUAD = 4 * ROWS


def ring(a):
    return min(a, 4 - a)


PEERS = sorted(((a, b) for a in range(4) for b in range(4) if a or b), key=lambda o: -ring(o[0]) - ring(o[1]))
NEAR = (3, -3, 2, -2, 1, -1)


def lse0(values):
    peak = jnp.max(values, axis=0, keepdims=True)
    return peak + jnp.log(jnp.sum(jnp.exp(values - peak), axis=0, keepdims=True))


def split3(v):
    hi = v.astype(BF16)
    rest = v - hi.astype(F32)
    mid = rest.astype(BF16)
    return hi, mid, (rest - mid.astype(F32)).astype(BF16)


def kernel(
    ps, pt, ls, lt, gp,
    out_f, out_t, out_m,
    xs, tb, gv, lv, lsv, y1, y3, yf, yt, aa, ltb, sc, rb, uu, lsum, cl, cb, vv, mp, tn, mm, mb, wt,
    loc, xs_s, xs_r, tb_s, tb_r, rb_s, rb_r, cb_s, cb_r, tn_s, tn_r, mb_s, mb_r,
):
    s = lax.axis_index("src")
    t = lax.axis_index("tgt")
    q = s >> 1
    zl = t >> 1
    c = t & 1
    z = (s & 1) * 8 + zl
    x = q >> 2
    y = q & 3
    me = z * 2 + c

    def peer(a, b):
        return ((x + a) & 3) * 4 + ((y + b) & 3)

    def plane_device(p):
        return (p * 2 + (s & 1), t)

    def column_device(to_z, to_c):
        return (q * 2 + (to_z >> 3), (to_z & 7) * 2 + to_c)

    def remote(src, dst, send, recv, device):
        return pltpu.make_async_remote_copy(
            src_ref=src, dst_ref=dst, send_sem=send, recv_sem=recv, device_id=device, device_id_type=MESH
        )

    def take(ref, recv):
        remote(ref, ref, recv, recv, plane_device(peer(1, 0))).wait_recv()

    def left(ref, send):
        remote(ref, ref, send, send, plane_device(peer(1, 0))).wait_send()

    barrier = pltpu.get_barrier_semaphore()
    for d in (4, -4, 3, -3, 2, -2, 1, -1):
        for to_c in range(2):
            pl.semaphore_signal(
                barrier, inc=1, device_id=column_device((z + d) & 15, to_c), device_id_type=MESH
            )
    for a, b in PEERS:
        pl.semaphore_signal(barrier, inc=1, device_id=plane_device(peer(a, b)), device_id_type=MESH)
    pl.semaphore_signal(barrier, inc=1, device_id=column_device(z, 1 - c), device_id_type=MESH)

    local = [
        pltpu.make_async_copy(gp, gv, loc.at[0]),
        pltpu.make_async_copy(lt, lv, loc.at[1]),
        pltpu.make_async_copy(pt.at[pl.ds(pl.multiple_of(q * SLICE, SLICE), SLICE)], tb.at[t, pl.ds(0, SLICE)], loc.at[2]),
        pltpu.make_async_copy(ps, xs.at[q], loc.at[3]),
        pltpu.make_async_copy(ls, lsv, loc.at[4]),
    ]
    for copy in local:
        copy.start()
    for copy in local:
        copy.wait()
    tb[pl.ds(t, 1), SLICE : SLICE + 1] = gv[pl.ds(q >> 2, 1), :][None]
    tb[pl.ds(t, 1), SLICE + 1 : SLICE + 2] = lv[pl.ds(q >> 2, 1), :][None]

    pl.semaphore_wait(barrier, 16 + 15 + 1)

    def send_targets(d, to_c):
        remote(
            tb.at[t], tb.at[t], tb_s.at[0], tb_r.at[abs(d)],
            column_device((z + d) & 15, (1 - c) if to_c is None else to_c),
        ).start()

    def send_points(a, b):
        remote(xs.at[q], xs.at[q], xs_s.at[0], xs_r.at[x], plane_device(peer(a, b))).start()

    todo = list(PEERS)
    for to_c in range(2):
        remote(
            tb.at[t], tb.at[t], tb_s.at[0], tb_r.at[4], column_device((z + 4 - 8 * c) & 15, to_c)
        ).start()
        send_points(*todo.pop(0))
    for d in NEAR:
        for to_c in range(2):
            send_targets(d, to_c)
            send_points(*todo.pop(0))
    send_points(*todo.pop(0))
    send_targets(0, None)

    lane = lax.broadcasted_iota(jnp.int32, (SLICE, 128), 1)
    sub = lax.broadcasted_iota(jnp.int32, (SLICE, 128), 0)
    mine = lane == sub + (q & 3) * SLICE

    def use_targets(off):
        for to_c in range(2):
            slot = ((zl + off) & 7) * 2 + to_c
            block = tb[pl.ds(slot, 1)][0]
            pts = block[0:SLICE]
            rows = pl.ds(pl.multiple_of(slot * SLICE, SLICE), SLICE)
            own = jnp.where(mine, 2.0 * block[SLICE : SLICE + 1], 0.0)
            a = jnp.sum(own - pts * pts, axis=1, keepdims=True)
            aa[rows, :] = jnp.broadcast_to(a, (SLICE, 128))
            hi, mid, lo = split3(2.0 * pts)
            yf[rows, :] = pts
            y1[rows, 0:128] = hi
            y1[rows, 128:256] = mid
            y3[rows, 0:128] = hi
            y3[rows, 128:256] = lo

    take(tb.at[0], tb_r.at[0])
    use_targets(0)
    for d in (1, 2, 3):
        take(tb.at[pl.ds(0, 4)], tb_r.at[d])
        use_targets(d)
        use_targets(8 - d)
    take(tb.at[pl.ds(0, 2)], tb_r.at[4])
    use_targets(4)

    for a in (0, 1, 3, 2):
        quad = (x + a) & 3
        take(xs.at[pl.ds(0, 4 if a else 3)], xs_r.at[quad])
        pts = xs[pl.ds(quad * 4, 4)].reshape(QUAD, 128)
        hi, mid, lo = split3(pts)

        def product(targets, first, second):
            return lax.dot_general(
                targets, jnp.concatenate([first, second], axis=1),
                (((1,), (1,)), ((), ())), preferred_element_type=F32,
            )

        prod = product(y3[...], lo, hi) + product(y1[...], mid, hi) + product(y1[...], hi, mid)
        score = prod + jnp.concatenate([aa[...], aa[...]], axis=1)
        sc[pl.ds(quad, 1)] = score[None]
        row = lse0(score)
        rb[pl.ds(q, 1), pl.ds(2 * quad, 1)] = row[:, 0:128][None]
        rb[pl.ds(q, 1), pl.ds(2 * quad + 1, 1)] = row[:, 128:256][None]

    half = (lax.broadcasted_iota(jnp.int32, (1, 128), 1) >> 6) == (q & 1)
    both = jnp.concatenate([lsv[...], lsv[...]], axis=1)
    rb[pl.ds(q, 1), 8:9] = jnp.where(half, both, 0.0)[None]
    for a, b in PEERS:
        remote(rb.at[q], rb.at[q], rb_s.at[0], rb_r.at[0], plane_device(peer(a, b))).start()

    for b in range(4):
        yb = yf[b * 128 : (b + 1) * 128, :].T
        hi = yb.astype(BF16)
        yt[0:128, b * 128 : (b + 1) * 128] = hi
        yt[128:256, b * 128 : (b + 1) * 128] = (yb - hi.astype(F32)).astype(BF16)
    for slot in range(16):
        l = jnp.sum(jnp.where(mine, tb[slot, SLICE + 1 : SLICE + 2], 0.0), axis=1, keepdims=True)
        ltb[slot * SLICE : (slot + 1) * SLICE, :] = jnp.broadcast_to(l, (SLICE, 128))
    own_points = xs[pl.ds(q, 1)][0]
    squares = jnp.concatenate([own_points * own_points, jnp.zeros((128 - ROWS, 128), F32)], axis=0)
    norm = jnp.sum(squares.T, axis=0, keepdims=True)

    take(rb.at[pl.ds(0, 15)], rb_r.at[0])
    rowlse = lse0(rb[:, 0:8])[0]
    uu[...] = rowlse
    for b in range(8):
        lsum[b : b + 1, :] = rb[2 * b, 8:9] + rb[2 * b + 1, 8:9]
    u = lsum[...] - rowlse

    def columns(j, carry):
        rows = pl.ds(pl.multiple_of(j * 32, 32), 32)
        vals = []
        for b in range(8):
            lanes = slice((b % 2) * 128, (b % 2) * 128 + 128)
            v = u[b : b + 1, :] + sc[b // 2, rows, lanes]
            sc[b // 2, rows, lanes] = v
            vals.append(v)
        peak = vals[0]
        for v in vals[1:]:
            peak = jnp.maximum(peak, v)
        total = jnp.exp(vals[0] - peak)
        for v in vals[1:]:
            total = total + jnp.exp(v - peak)
        cl[rows, :] = peak + jnp.log(total)
        return carry

    lax.fori_loop(0, 16, columns, 0)
    for b in range(4):
        cb[pl.ds(me, 1), b : b + 1] = lse0(cl[b * 128 : (b + 1) * 128, :].T)[None]

    def send_columns(d, to_c):
        remote(cb.at[me], cb.at[me], cb_s.at[0], cb_r.at[0], column_device((z + d) & 15, to_c)).start()

    for d in (8, 7, -7, 6, -6, 5, -5, 4, -4, 3, -3, 2, -2, 1, -1):
        for to_c in range(2):
            send_columns(d, to_c)
    send_columns(0, 1 - c)

    own_lse = uu[pl.ds(q >> 1, 1), :]
    own_lse = jnp.where(q & 1 == 0, own_lse, pltpu.roll(own_lse, 64, 1))
    out_f[...] = 0.5 * (lsv[...] + norm[:, 0:ROWS] - own_lse[:, 0:ROWS])

    take(cb.at[pl.ds(0, 31)], cb_r.at[0])
    collse = lse0(cb[...])[0]
    for b in range(4):
        mp[b] = collse[b : b + 1, :]
        spread = jnp.broadcast_to(collse[b : b + 1, :], (128, 128)).T
        vv[b * 128 : (b + 1) * 128, :] = ltb[b * 128 : (b + 1) * 128, :] - spread

    for a in (2, 1, 3, 0):
        quad = (x + a) & 3
        val = sc[pl.ds(quad, 1)][0] + jnp.concatenate([vv[...], vv[...]], axis=1)
        w = jnp.exp(val)
        total = jnp.sum(w, axis=0, keepdims=True)
        hi = w.astype(BF16)
        lo = (w - hi.astype(F32)).astype(BF16)
        first = jnp.dot(yt[...], hi, preferred_element_type=F32)
        second = jnp.dot(yt[0:128, :], lo, preferred_element_type=F32)
        n = first[0:128] + first[128:256] + second
        n = jnp.concatenate([n[:, 0:128].T, n[:, 128:256].T], axis=0)
        for h in range(4):
            part = jnp.concatenate([n[h * ROWS : (h + 1) * ROWS], total[:, (h // 2) * 128 : (h // 2) * 128 + 128]], axis=0)
            mm[pl.ds(quad * 4 + h, 1)] = part[None]
        for b in (2, 1, 3, 0):
            if a or b:
                p = peer(a, b)
                remote(mm.at[p], mb.at[q], mb_s.at[0], mb_r.at[x], plane_device(p)).start()

    tn[pl.ds(q, 1)] = mp[pl.ds(t >> 2, 1)]
    for a, b in PEERS:
        remote(tn.at[q], tn.at[q], tn_s.at[0], tn_r.at[0], plane_device(peer(a, b))).start()
    take(tn.at[pl.ds(0, 15)], tn_r.at[0])
    pieces = tn[...].reshape(16, 128)
    lane16 = lax.broadcasted_iota(jnp.int32, (16, 128), 1) >> 5
    sub16 = lax.broadcasted_iota(jnp.int32, (16, 128), 0) & 3
    whole = jnp.zeros((16, 128), F32)
    for k in range(4):
        turned = pltpu.roll(pieces, ((k - t) & 3) * SLICE, 1)
        whole = whole + jnp.where((lane16 == k) & (sub16 == k), turned, 0.0)
    for b in range(4):
        row = jnp.sum(whole[4 * b : 4 * b + 4], axis=0, keepdims=True)
        out_t[b : b + 1, :] = gv[b : b + 1, :] + 0.5 * (lv[b : b + 1, :] - row)

    mb[pl.ds(q, 1)] = mm[pl.ds(q, 1)]
    total = jnp.zeros((ROWS + 1, 128), F32)
    for a in (0, 1, 3, 2):
        quad = (x + a) & 3
        take(mb.at[pl.ds(0, 4 if a else 3)], mb_r.at[quad])
        got = mb[pl.ds(quad * 4, 4)]
        total = total + ((got[0] + got[1]) + (got[2] + got[3]))
    wt[...] = jnp.broadcast_to(1.0 / total[ROWS : ROWS + 1], (128, 128)).T
    out_m[...] = total[0:ROWS] * wt[pl.ds(pl.multiple_of((q & 1) * ROWS, ROWS), ROWS), :]

    left(tb.at[pl.ds(0, 15)], tb_s.at[0])
    left(xs.at[pl.ds(0, 15)], xs_s.at[0])
    left(rb.at[pl.ds(0, 15)], rb_s.at[0])
    left(cb.at[pl.ds(0, 31)], cb_s.at[0])
    left(tn.at[pl.ds(0, 15)], tn_s.at[0])
    left(mm.at[pl.ds(0, 15)], mb_s.at[0])


def finish(f_ref, t_ref, m_ref, out_f, out_t, out_m):
    out_f[...] = f_ref[...]
    out_t[...] = t_ref[...]
    out_m[...] = m_ref[...]


def shards(points_src, points_tgt, log_source, log_target, target_potential):
    vmem = pl.BlockSpec(memory_space=pltpu.VMEM)
    hbm = pl.BlockSpec(memory_space=pltpu.HBM)
    dma = pltpu.SemaphoreType.DMA
    shapes = (
        jax.ShapeDtypeStruct((1, ROWS), F32),
        jax.ShapeDtypeStruct((4, 128), F32),
        jax.ShapeDtypeStruct((ROWS, 128), F32),
    )
    results = pl.pallas_call(
        kernel,
        name="sinkhorn",
        out_shape=shapes,
        in_specs=[hbm] * 5,
        out_specs=(vmem,) * 3,
        scratch_shapes=[
            pltpu.VMEM((16, ROWS, 128), F32),
            pltpu.VMEM((16, SLICE + 2, 128), F32),
            pltpu.VMEM((4, 128), F32),
            pltpu.VMEM((4, 128), F32),
            pltpu.VMEM((1, ROWS), F32),
            pltpu.VMEM((512, 256), BF16),
            pltpu.VMEM((512, 256), BF16),
            pltpu.VMEM((512, 128), F32),
            pltpu.VMEM((256, 512), BF16),
            pltpu.VMEM((512, 128), F32),
            pltpu.VMEM((512, 128), F32),
            pltpu.VMEM((4, 512, QUAD), F32),
            pltpu.VMEM((16, 9, 128), F32),
            pltpu.VMEM((8, 128), F32),
            pltpu.VMEM((8, 128), F32),
            pltpu.VMEM((512, 128), F32),
            pltpu.VMEM((32, 4, 128), F32),
            pltpu.VMEM((512, 128), F32),
            pltpu.VMEM((4, 1, 128), F32),
            pltpu.VMEM((16, 1, 128), F32),
            pltpu.VMEM((16, ROWS + 1, 128), F32),
            pltpu.VMEM((16, ROWS + 1, 128), F32),
            pltpu.VMEM((128, 128), F32),
            dma((5,)),
            dma((1,)), dma((4,)),
            dma((1,)), dma((5,)),
            dma((1,)), dma((1,)),
            dma((1,)), dma((1,)),
            dma((1,)), dma((1,)),
            dma((1,)), dma((4,)),
        ],
        compiler_params=pltpu.CompilerParams(
            collective_id=0, has_side_effects=True, vmem_limit_bytes=56 * 2**20
        ),
    )(
        points_src,
        points_tgt,
        log_source.reshape(1, ROWS),
        log_target.reshape(4, 128),
        target_potential.reshape(4, 128),
    )
    source_potential, target_new, mapped = pl.pallas_call(
        finish, name="finish", out_shape=shapes, in_specs=[vmem] * 3, out_specs=(vmem,) * 3
    )(*results)
    return source_potential.reshape(ROWS), target_new.reshape(512), mapped


def solution(mesh):
    return jax.shard_map(
        shards,
        mesh=mesh,
        in_specs=(P(("src", "tgt"), None), P("tgt", None), P(("src", "tgt")), P("tgt"), P("tgt")),
        out_specs=(P(("src", "tgt")), P("tgt"), P(("src", "tgt"), None)),
        check_vma=False,
    )
```

```python
import jax
import jax.numpy as jnp
from jax import lax
from jax.experimental import pallas as pl
from jax.experimental.pallas import tpu as pltpu
from jax.sharding import PartitionSpec as P

MESH = pl.DeviceIdType.MESH
F32 = jnp.float32
BF16 = jnp.bfloat16
ROWS = 64
SLICE = 32
QUAD = 4 * ROWS


def ring(a):
    return min(a, 4 - a)


PEERS = sorted(((a, b) for a in range(4) for b in range(4) if a or b), key=lambda o: -ring(o[0]) - ring(o[1]))

GATHER_GROUPS = ((0, 1, 3, 2),)
MAP_GROUPS = ((2, 1, 3, 0),)


LOG2E = 1.4426950408889634
LN2 = 0.6931471805599453


def lse0(values):
    peak = jnp.max(values, axis=0, keepdims=True)
    return peak + LOG2E * jnp.log(jnp.sum(jnp.exp2(values - peak), axis=0, keepdims=True))


def split3(v):
    hi = v.astype(BF16)
    rest = v - hi.astype(F32)
    mid = rest.astype(BF16)
    return hi, mid, (rest - mid.astype(F32)).astype(BF16)


def kernel(
    ps, pt, ls, lt, gp,
    out_f, out_t, out_m,
    xs, tb, gv, lv, lsv, y1, y3, yf, yt, aa, ltb, sc, rb, uu, lsum, cl, cb, vv, mp, mm, mb, wt,
    loc, xs_s, xs_r, tb_s, tb_r, fw_r, rb_s, rb_r, cb_s, cb_r, mb_s, mb_r,
):
    s = lax.axis_index("src")
    t = lax.axis_index("tgt")
    q = s >> 1
    zl = t >> 1
    c = t & 1
    z = (s & 1) * 8 + zl
    x = q >> 2
    y = q & 3
    me = z * 2 + c

    def peer(a, b):
        return ((x + a) & 3) * 4 + ((y + b) & 3)

    def plane_device(p):
        return (p * 2 + (s & 1), t)

    def column_device(to_z, to_c):
        return (q * 2 + (to_z >> 3), (to_z & 7) * 2 + to_c)

    def remote(src, dst, send, recv, device):
        return pltpu.make_async_remote_copy(
            src_ref=src, dst_ref=dst, send_sem=send, recv_sem=recv, device_id=device, device_id_type=MESH
        )

    def take(ref, recv):
        remote(ref, ref, recv, recv, plane_device(peer(1, 0))).wait_recv()

    def left(ref, send):
        remote(ref, ref, send, send, plane_device(peer(1, 0))).wait_send()

    barrier = pltpu.get_barrier_semaphore()
    for d in (4, -4, 3, -3, 2, -2, 1, -1):
        for to_c in range(2):
            pl.semaphore_signal(
                barrier, inc=1, device_id=column_device((z + d) & 15, to_c), device_id_type=MESH
            )
    for a, b in PEERS:
        pl.semaphore_signal(barrier, inc=1, device_id=plane_device(peer(a, b)), device_id_type=MESH)
    pl.semaphore_signal(barrier, inc=1, device_id=column_device(z, 1 - c), device_id_type=MESH)

    local = [
        pltpu.make_async_copy(gp, gv, loc.at[0]),
        pltpu.make_async_copy(lt, lv, loc.at[1]),
        pltpu.make_async_copy(pt.at[pl.ds(pl.multiple_of(q * SLICE, SLICE), SLICE)], tb.at[t, pl.ds(0, SLICE)], loc.at[2]),
        pltpu.make_async_copy(ps, xs.at[q], loc.at[3]),
        pltpu.make_async_copy(ls, lsv, loc.at[4]),
    ]
    for copy in local:
        copy.start()
    for copy in local:
        copy.wait()
    tb[pl.ds(t, 1), SLICE : SLICE + 1] = gv[pl.ds(q >> 2, 1), :][None]
    tb[pl.ds(t, 1), SLICE + 1 : SLICE + 2] = lv[pl.ds(q >> 2, 1), :][None]

    pl.semaphore_wait(barrier, 16 + 15 + 1)

    def send_targets(slot, recv, device):
        remote(tb.at[slot], tb.at[slot], tb_s.at[0], recv, device).start()

    def send_points(a, b):
        remote(xs.at[q], xs.at[q], xs_s.at[0], xs_r.at[x], plane_device(peer(a, b))).start()

    sibling = column_device(z, 1 - c)
    send_targets(t, tb_r.at[3], column_device((z + 4 - 8 * c) & 15, c))
    for d, offsets in zip((3, -3, 2, -2, 1, -1), PEERS[0:6]):
        send_targets(t, tb_r.at[abs(d) - 1], column_device((z + d) & 15, c))
        send_points(*offsets)
    send_targets(t, fw_r.at[0], sibling)
    for offsets in PEERS[6:]:
        send_points(*offsets)

    lane = lax.broadcasted_iota(jnp.int32, (SLICE, 128), 1)
    sub = lax.broadcasted_iota(jnp.int32, (SLICE, 128), 0)
    mine = lane == sub + (q & 3) * SLICE

    def use_targets(slot):
        block = tb[pl.ds(slot, 1)][0]
        pts = block[0:SLICE]
        rows = pl.ds(pl.multiple_of(slot * SLICE, SLICE), SLICE)
        own = jnp.where(mine, 2.0 * block[SLICE : SLICE + 1], 0.0)
        a = LOG2E * jnp.sum(own - pts * pts, axis=1, keepdims=True)
        aa[rows, :] = jnp.broadcast_to(a, (SLICE, 128))
        hi, mid, lo = split3((2.0 * LOG2E) * pts)
        yf[rows, :] = pts
        y1[rows, 0:128] = hi
        y1[rows, 128:256] = mid
        y3[rows, 0:128] = hi
        y3[rows, 128:256] = lo

    def offsets_at(d):
        return (d, 8 - d) if d % 4 else (d,)

    def use_forwarded(d):
        take(tb.at[pl.ds(0, len(offsets_at(d)))], fw_r.at[d])
        for off in offsets_at(d):
            use_targets(((zl + off) & 7) * 2 + 1 - c)

    for d in (1, 2, 3, 4):
        take(tb.at[pl.ds(0, len(offsets_at(d)))], tb_r.at[d - 1])
        slots = [((zl + off) & 7) * 2 + c for off in offsets_at(d)]
        for slot in slots:
            send_targets(slot, fw_r.at[d], sibling)
        if d > 1:
            take(tb.at[pl.ds(0, len(offsets_at(d - 1)))], fw_r.at[d - 1])
    take(tb.at[0], fw_r.at[0])
    take(tb.at[0], fw_r.at[4])
    for slot in range(16):
        use_targets(slot)

    def product(targets, first, second):
        return lax.dot_general(
            targets, jnp.concatenate([first, second], axis=1),
            (((1,), (1,)), ((), ())), preferred_element_type=F32,
        )

    for group in GATHER_GROUPS:
        for a in group:
            take(xs.at[pl.ds(0, 4 if a else 3)], xs_r.at[(x + a) & 3])
        for a in group:
            quad = (x + a) & 3
            hi, mid, lo = split3(xs[pl.ds(quad * 4, 4)].reshape(QUAD, 128))
            prod = product(y3[...], lo, hi) + product(y1[...], mid, hi) + product(y1[...], hi, mid)
            score = prod + jnp.concatenate([aa[...], aa[...]], axis=1)
            sc[pl.ds(quad, 1)] = score[None]
            row = lse0(score)
            rb[pl.ds(q, 1), pl.ds(2 * quad, 1)] = row[:, 0:128][None]
            rb[pl.ds(q, 1), pl.ds(2 * quad + 1, 1)] = row[:, 128:256][None]

    half = (lax.broadcasted_iota(jnp.int32, (1, 128), 1) >> 6) == (q & 1)
    both = jnp.concatenate([lsv[...], lsv[...]], axis=1)
    rb[pl.ds(q, 1), 8:9] = jnp.where(half, both, 0.0)[None]
    for a, b in PEERS:
        remote(rb.at[q], rb.at[q], rb_s.at[0], rb_r.at[0], plane_device(peer(a, b))).start()

    for b in range(4):
        yb = yf[b * 128 : (b + 1) * 128, :].T
        hi = yb.astype(BF16)
        yt[0:128, b * 128 : (b + 1) * 128] = hi
        yt[128:256, b * 128 : (b + 1) * 128] = (yb - hi.astype(F32)).astype(BF16)
    for slot in range(16):
        l = LOG2E * jnp.sum(jnp.where(mine, tb[slot, SLICE + 1 : SLICE + 2], 0.0), axis=1, keepdims=True)
        ltb[slot * SLICE : (slot + 1) * SLICE, :] = jnp.broadcast_to(l, (SLICE, 128))
    own_points = xs[pl.ds(q, 1)][0]
    squares = jnp.concatenate([own_points * own_points, jnp.zeros((128 - ROWS, 128), F32)], axis=0)
    norm = jnp.sum(squares.T, axis=0, keepdims=True)

    take(rb.at[pl.ds(0, 15)], rb_r.at[0])
    rowlse = lse0(rb[:, 0:8])[0]
    uu[...] = rowlse
    for b in range(8):
        lsum[b : b + 1, :] = rb[2 * b, 8:9] + rb[2 * b + 1, 8:9]
    u = LOG2E * lsum[...] - rowlse

    def columns(j, carry):
        rows = pl.ds(pl.multiple_of(j * 32, 32), 32)
        vals = []
        for b in range(8):
            lanes = slice((b % 2) * 128, (b % 2) * 128 + 128)
            v = u[b : b + 1, :] + sc[b // 2, rows, lanes]
            sc[b // 2, rows, lanes] = v
            vals.append(v)
        peak = vals[0]
        for v in vals[1:]:
            peak = jnp.maximum(peak, v)
        total = jnp.exp2(vals[0] - peak)
        for v in vals[1:]:
            total = total + jnp.exp2(v - peak)
        cl[rows, :] = peak + LOG2E * jnp.log(total)
        return carry

    lax.fori_loop(0, 16, columns, 0, unroll=True)
    for b in range(4):
        cb[pl.ds(me, 1), b : b + 1] = lse0(cl[b * 128 : (b + 1) * 128, :].T)[None]

    def send_columns(d, to_c):
        remote(cb.at[me], cb.at[me], cb_s.at[0], cb_r.at[0], column_device((z + d) & 15, to_c)).start()

    for d in (8, 7, -7, 6, -6, 5, -5, 4, -4, 3, -3, 2, -2, 1, -1):
        for to_c in range(2):
            send_columns(d, to_c)
    send_columns(0, 1 - c)

    own_lse = uu[pl.ds(q >> 1, 1), :]
    own_lse = jnp.where(q & 1 == 0, own_lse, pltpu.roll(own_lse, 64, 1))
    out_f[...] = 0.5 * (lsv[...] + norm[:, 0:ROWS] - LN2 * own_lse[:, 0:ROWS])

    take(cb.at[pl.ds(0, 31)], cb_r.at[0])
    collse = lse0(cb[...])[0]
    for b in range(4):
        mp[b : b + 1, :] = collse[b : b + 1, :]
        spread = jnp.broadcast_to(collse[b : b + 1, :], (128, 128)).T
        vv[b * 128 : (b + 1) * 128, :] = ltb[b * 128 : (b + 1) * 128, :] - spread

    new_row = mp[pl.ds(t >> 2, 1), :]

    for group in MAP_GROUPS:
        for a in group:
            quad = (x + a) & 3
            w = jnp.exp2(sc[pl.ds(quad, 1)][0] + jnp.concatenate([vv[...], vv[...]], axis=1))
            total = jnp.sum(w, axis=0, keepdims=True)
            hi = w.astype(BF16)
            lo = (w - hi.astype(F32)).astype(BF16)
            first = jnp.dot(yt[...], hi, preferred_element_type=F32)
            second = jnp.dot(yt[0:128, :], lo, preferred_element_type=F32)
            n = first[0:128] + first[128:256] + second
            n = jnp.concatenate([n[:, 0:128].T, n[:, 128:256].T], axis=0)
            for h in range(4):
                lanes = slice((h // 2) * 128, (h // 2) * 128 + 128)
                part = jnp.concatenate([n[h * ROWS : (h + 1) * ROWS], total[:, lanes], new_row], axis=0)
                mm[pl.ds(quad * 4 + h, 1)] = part[None]
        for a in group:
            for b in (2, 1, 3, 0):
                if a or b:
                    p = peer(a, b)
                    remote(mm.at[p], mb.at[q], mb_s.at[0], mb_r.at[x], plane_device(p)).start()

    mb[pl.ds(q, 1)] = mm[pl.ds(q, 1)]
    total = jnp.zeros((ROWS + 1, 128), F32)
    for a in (0, 1, 3, 2):
        quad = (x + a) & 3
        take(mb.at[pl.ds(0, 4 if a else 3)], mb_r.at[quad])
        got = mb[pl.ds(quad * 4, 4), 0 : ROWS + 1]
        total = total + ((got[0] + got[1]) + (got[2] + got[3]))
    wt[...] = jnp.broadcast_to(1.0 / total[ROWS : ROWS + 1], (128, 128)).T
    out_m[...] = total[0:ROWS] * wt[pl.ds(pl.multiple_of((q & 1) * ROWS, ROWS), ROWS), :]

    pieces = mb[:, ROWS + 1 : ROWS + 2].reshape(16, 128)
    lane16 = lax.broadcasted_iota(jnp.int32, (16, 128), 1) >> 5
    sub16 = lax.broadcasted_iota(jnp.int32, (16, 128), 0) & 3
    whole = jnp.zeros((16, 128), F32)
    for k in range(4):
        turned = pltpu.roll(pieces, ((k - t) & 3) * SLICE, 1)
        whole = whole + jnp.where((lane16 == k) & (sub16 == k), turned, 0.0)
    for b in range(4):
        row = jnp.sum(whole[4 * b : 4 * b + 4], axis=0, keepdims=True)
        out_t[b : b + 1, :] = gv[b : b + 1, :] + 0.5 * (lv[b : b + 1, :] - LN2 * row)

    left(tb.at[pl.ds(0, 15)], tb_s.at[0])
    left(xs.at[pl.ds(0, 15)], xs_s.at[0])
    left(rb.at[pl.ds(0, 15)], rb_s.at[0])
    left(cb.at[pl.ds(0, 31)], cb_s.at[0])
    left(mm.at[pl.ds(0, 15)], mb_s.at[0])


def finish(f_ref, t_ref, m_ref, out_f, out_t, out_m):
    out_f[...] = f_ref[...]
    out_t[...] = t_ref[...]
    out_m[...] = m_ref[...]


def shards(points_src, points_tgt, log_source, log_target, target_potential):
    vmem = pl.BlockSpec(memory_space=pltpu.VMEM)
    hbm = pl.BlockSpec(memory_space=pltpu.HBM)
    dma = pltpu.SemaphoreType.DMA
    shapes = (
        jax.ShapeDtypeStruct((1, ROWS), F32),
        jax.ShapeDtypeStruct((4, 128), F32),
        jax.ShapeDtypeStruct((ROWS, 128), F32),
    )
    results = pl.pallas_call(
        kernel,
        name="sinkhorn",
        out_shape=shapes,
        in_specs=[hbm] * 5,
        out_specs=(vmem,) * 3,
        scratch_shapes=[
            pltpu.VMEM((16, ROWS, 128), F32),
            pltpu.VMEM((16, SLICE + 2, 128), F32),
            pltpu.VMEM((4, 128), F32),
            pltpu.VMEM((4, 128), F32),
            pltpu.VMEM((1, ROWS), F32),
            pltpu.VMEM((512, 256), BF16),
            pltpu.VMEM((512, 256), BF16),
            pltpu.VMEM((512, 128), F32),
            pltpu.VMEM((256, 512), BF16),
            pltpu.VMEM((512, 128), F32),
            pltpu.VMEM((512, 128), F32),
            pltpu.VMEM((4, 512, QUAD), F32),
            pltpu.VMEM((16, 9, 128), F32),
            pltpu.VMEM((8, 128), F32),
            pltpu.VMEM((8, 128), F32),
            pltpu.VMEM((512, 128), F32),
            pltpu.VMEM((32, 4, 128), F32),
            pltpu.VMEM((512, 128), F32),
            pltpu.VMEM((4, 128), F32),
            pltpu.VMEM((16, ROWS + 2, 128), F32),
            pltpu.VMEM((16, ROWS + 2, 128), F32),
            pltpu.VMEM((128, 128), F32),
            dma((5,)),
            dma((1,)), dma((4,)),
            dma((1,)), dma((4,)), dma((5,)),
            dma((1,)), dma((1,)),
            dma((1,)), dma((1,)),
            dma((1,)), dma((4,)),
        ],
        compiler_params=pltpu.CompilerParams(
            collective_id=0, has_side_effects=True, vmem_limit_bytes=56 * 2**20
        ),
    )(
        points_src,
        points_tgt,
        log_source.reshape(1, ROWS),
        log_target.reshape(4, 128),
        target_potential.reshape(4, 128),
    )
    source_potential, target_new, mapped = pl.pallas_call(
        finish, name="finish", out_shape=shapes, in_specs=[vmem] * 3, out_specs=(vmem,) * 3
    )(*results)
    return source_potential.reshape(ROWS), target_new.reshape(512), mapped


def solution(mesh):
    return jax.shard_map(
        shards,
        mesh=mesh,
        in_specs=(P(("src", "tgt"), None), P("tgt", None), P(("src", "tgt")), P("tgt"), P("tgt")),
        out_specs=(P(("src", "tgt")), P("tgt"), P(("src", "tgt"), None)),
        check_vma=False,
    )
```

```python
import jax
import jax.numpy as jnp
from jax import lax
from jax.experimental import pallas as pl
from jax.experimental.pallas import tpu as pltpu
from jax.sharding import PartitionSpec as P

MESH = pl.DeviceIdType.MESH
F32 = jnp.float32
BF16 = jnp.bfloat16
ROWS = 64
HALF = 32
SLICE = 32
QUAD = 4 * ROWS


def ring(a):
    return min(a, 4 - a)


PEERS = sorted(((a, b) for a in range(4) for b in range(4) if a or b), key=lambda o: -ring(o[0]) - ring(o[1]))

LOG2E = 1.4426950408889634
LN2 = 0.6931471805599453


def lse0(values):
    peak = jnp.max(values, axis=0, keepdims=True)
    return peak + LOG2E * jnp.log(jnp.sum(jnp.exp2(values - peak), axis=0, keepdims=True))


def split3(v):
    hi = v.astype(BF16)
    rest = v - hi.astype(F32)
    mid = rest.astype(BF16)
    return hi, mid, (rest - mid.astype(F32)).astype(BF16)


def gather_lanes(pieces, group):
    lane = lax.broadcasted_iota(jnp.int32, (16, 128), 1) >> 5
    row = lax.broadcasted_iota(jnp.int32, (16, 128), 0) & 3
    whole = jnp.zeros((16, 128), F32)
    for k in range(4):
        turned = pltpu.roll(pieces, ((k - group) & 3) * SLICE, 1)
        whole = whole + jnp.where((lane == k) & (row == k), turned, 0.0)
    return jnp.concatenate([jnp.sum(whole[4 * b : 4 * b + 4], axis=0, keepdims=True) for b in range(4)], axis=0)


def kernel(
    ps, pt, ls, lt, gp,
    out_f, out_t, out_m,
    xs, tb, gv, lv, lsv, y1, y3, yf, yt, aa, sc, eh, el, fs, rb, uu, lsum, cl, cb, mp, mm, mb, wt,
    loc, xs_s, xs_r, tb_s, tb_r, fw_r, rb_s, rb_r, cb_s, cb_r, mb_s, mb_r,
):
    s = lax.axis_index("src")
    t = lax.axis_index("tgt")
    q = s >> 1
    zl = t >> 1
    c = t & 1
    z = (s & 1) * 8 + zl
    x = q >> 2
    y = q & 3
    me = z * 2 + c

    def peer(a, b):
        return ((x + a) & 3) * 4 + ((y + b) & 3)

    def plane_device(p):
        return (p * 2 + (s & 1), t)

    def column_device(to_z, to_c):
        return (q * 2 + (to_z >> 3), (to_z & 7) * 2 + to_c)

    def remote(src, dst, send, recv, device):
        return pltpu.make_async_remote_copy(
            src_ref=src, dst_ref=dst, send_sem=send, recv_sem=recv, device_id=device, device_id_type=MESH
        )

    def take(ref, recv):
        remote(ref, ref, recv, recv, plane_device(peer(1, 0))).wait_recv()

    def left(ref, send):
        remote(ref, ref, send, send, plane_device(peer(1, 0))).wait_send()

    barrier = pltpu.get_barrier_semaphore()
    for d in (4, -4, 3, -3, 2, -2, 1, -1):
        for to_c in range(2):
            pl.semaphore_signal(
                barrier, inc=1, device_id=column_device((z + d) & 15, to_c), device_id_type=MESH
            )
    for a, b in PEERS:
        pl.semaphore_signal(barrier, inc=1, device_id=plane_device(peer(a, b)), device_id_type=MESH)
    pl.semaphore_signal(barrier, inc=1, device_id=column_device(z, 1 - c), device_id_type=MESH)

    local = [
        pltpu.make_async_copy(gp, gv, loc.at[0]),
        pltpu.make_async_copy(lt, lv, loc.at[1]),
        pltpu.make_async_copy(pt.at[pl.ds(pl.multiple_of(q * SLICE, SLICE), SLICE)], tb.at[t, pl.ds(0, SLICE)], loc.at[2]),
        pltpu.make_async_copy(ps, xs.at[q], loc.at[3]),
        pltpu.make_async_copy(ls, lsv, loc.at[4]),
    ]
    for copy in local:
        copy.start()
    for copy in local:
        copy.wait()
    tb[pl.ds(t, 1), SLICE : SLICE + 1] = gv[pl.ds(q >> 2, 1), :][None]
    tb[pl.ds(t, 1), SLICE + 1 : SLICE + 2] = lv[pl.ds(q >> 2, 1), :][None]

    pl.semaphore_wait(barrier, 16 + 15 + 1)

    def send_targets(slot, recv, device):
        remote(tb.at[slot], tb.at[slot], tb_s.at[0], recv, device).start()

    def send_half(p, h, recv, to):
        part = xs.at[p, pl.ds(h * HALF, HALF)]
        remote(part, part, xs_s.at[0], recv, plane_device(to)).start()

    def pass_on(p, h):
        for k in (2, 1, 3):
            send_half(p, h, xs_r.at[0], peer(k, 0) if h else peer(0, k))

    sibling = column_device(z, 1 - c)
    send_targets(t, tb_r.at[3], column_device((z + 4 - 8 * c) & 15, c))
    for k in (2, 1, 3):
        send_half(q, 0, xs_r.at[k], peer(k, 0))
        send_half(q, 1, xs_r.at[3 + k], peer(0, k))
    for d in (3, -3, 2, -2):
        send_targets(t, tb_r.at[abs(d) - 1], column_device((z + d) & 15, c))
    pass_on(q, 0)
    pass_on(q, 1)
    for d in (1, -1):
        send_targets(t, tb_r.at[abs(d) - 1], column_device((z + d) & 15, c))
    send_targets(t, fw_r.at[0], sibling)
    half_block = xs.at[0, pl.ds(0, HALF)]
    for k in (1, 3, 2):
        take(half_block, xs_r.at[k])
        pass_on(peer(-k, 0), 0)
        take(half_block, xs_r.at[3 + k])
        pass_on(peer(0, -k), 1)

    lane = lax.broadcasted_iota(jnp.int32, (SLICE, 128), 1)
    sub = lax.broadcasted_iota(jnp.int32, (SLICE, 128), 0)
    mine = lane == sub + (q & 3) * SLICE

    def use_targets(slot):
        block = tb[pl.ds(slot, 1)][0]
        pts = block[0:SLICE]
        rows = pl.ds(pl.multiple_of(slot * SLICE, SLICE), SLICE)
        own = jnp.where(mine, 2.0 * block[SLICE : SLICE + 1], 0.0)
        a = LOG2E * jnp.sum(own - pts * pts, axis=1, keepdims=True)
        aa[rows, :] = jnp.broadcast_to(a, (SLICE, 128))
        hi, mid, lo = split3((2.0 * LOG2E) * pts)
        yf[rows, :] = pts
        y1[rows, 0:128] = hi
        y1[rows, 128:256] = mid
        y3[rows, 0:128] = hi
        y3[rows, 128:256] = lo

    def offsets_at(d):
        return (d, 8 - d) if d % 4 else (d,)

    def use_forwarded(d):
        take(tb.at[pl.ds(0, len(offsets_at(d)))], fw_r.at[d])
        for off in offsets_at(d):
            use_targets(((zl + off) & 7) * 2 + 1 - c)

    for d in (1, 2, 3, 4):
        take(tb.at[pl.ds(0, len(offsets_at(d)))], tb_r.at[d - 1])
        slots = [((zl + off) & 7) * 2 + c for off in offsets_at(d)]
        for slot in slots:
            send_targets(slot, fw_r.at[d], sibling)
        if d > 1:
            take(tb.at[pl.ds(0, len(offsets_at(d - 1)))], fw_r.at[d - 1])
    take(tb.at[0], fw_r.at[0])
    take(tb.at[0], fw_r.at[4])
    for slot in range(16):
        use_targets(slot)

    def product(targets, first, second):
        return lax.dot_general(
            targets, jnp.concatenate([first, second], axis=1),
            (((1,), (1,)), ((), ())), preferred_element_type=F32,
        )

    take(xs.at[pl.ds(0, 12)], xs_r.at[0])
    for quad in range(4):
        hi, mid, lo = split3(xs[quad * 4 : quad * 4 + 4].reshape(QUAD, 128))
        prod = product(y3[...], lo, hi) + product(y1[...], mid, hi) + product(y1[...], hi, mid)
        score = prod + jnp.concatenate([aa[...], aa[...]], axis=1)
        sc[quad] = score
        row = lse0(score)
        rb[pl.ds(q, 1), 2 * quad : 2 * quad + 1] = row[:, 0:128][None]
        rb[pl.ds(q, 1), 2 * quad + 1 : 2 * quad + 2] = row[:, 128:256][None]

    half = (lax.broadcasted_iota(jnp.int32, (1, 128), 1) >> 6) == (q & 1)
    both = jnp.concatenate([lsv[...], lsv[...]], axis=1)
    rb[pl.ds(q, 1), 8:9] = jnp.where(half, both, 0.0)[None]
    for a, b in PEERS:
        remote(rb.at[q], rb.at[q], rb_s.at[0], rb_r.at[0], plane_device(peer(a, b))).start()

    for b in range(4):
        yt[:, b * 128 : (b + 1) * 128] = yf[b * 128 : (b + 1) * 128, :].T
    log_target = LOG2E * gather_lanes(tb[:, SLICE + 1 : SLICE + 2].reshape(16, 128), q & 3)
    own_points = xs[pl.ds(q, 1)][0]
    squares = jnp.concatenate([own_points * own_points, jnp.zeros((128 - ROWS, 128), F32)], axis=0)
    norm = jnp.sum(squares.T, axis=0, keepdims=True)

    take(rb.at[pl.ds(0, 15)], rb_r.at[0])
    rowlse = lse0(rb[:, 0:8])[0]
    uu[...] = rowlse
    for b in range(8):
        lsum[b : b + 1, :] = rb[2 * b, 8:9] + rb[2 * b + 1, 8:9]
    u = LOG2E * lsum[...] - rowlse

    def columns(j, carry):
        rows = pl.ds(pl.multiple_of(j * 32, 32), 32)
        vals = []
        for b in range(8):
            lanes = slice((b % 2) * 128, (b % 2) * 128 + 128)
            v = u[b : b + 1, :] + sc[b // 2, rows, lanes]
            sc[b // 2, rows, lanes] = v
            vals.append(v)
        peak = vals[0]
        for v in vals[1:]:
            peak = jnp.maximum(peak, v)
        total = jnp.exp2(vals[0] - peak)
        for v in vals[1:]:
            total = total + jnp.exp2(v - peak)
        cl[rows, :] = peak + LOG2E * jnp.log(total)
        return carry

    lax.fori_loop(0, 16, columns, 0, unroll=True)
    tops = []
    for b in range(4):
        turned = cl[b * 128 : (b + 1) * 128, :].T
        tops.append(jnp.max(turned, axis=0, keepdims=True))
        cb[pl.ds(me, 1), b : b + 1] = lse0(turned)[None]

    def send_columns(d, to_c):
        remote(cb.at[me], cb.at[me], cb_s.at[0], cb_r.at[0], column_device((z + d) & 15, to_c)).start()

    for d in (8, 7, -7, 6, -6, 5, -5, 4, -4, 3, -3, 2, -2, 1, -1):
        for to_c in range(2):
            send_columns(d, to_c)
    send_columns(0, 1 - c)

    own_lse = uu[pl.ds(q >> 1, 1), :]
    own_lse = jnp.where(q & 1 == 0, own_lse, pltpu.roll(own_lse, 64, 1))
    out_f[...] = 0.5 * (lsv[...] + norm[:, 0:ROWS] - LN2 * own_lse[:, 0:ROWS])

    def weights(j, carry):
        rows = pl.ds(pl.multiple_of(j * 32, 32), 32)
        top = jnp.max(cl[rows, :], axis=1, keepdims=True)
        for quad in range(4):
            w = jnp.exp2(sc[quad, rows, :] - top)
            hi = w.astype(BF16)
            eh[quad, rows, :] = hi
            el[quad, rows, :] = (w - hi.astype(F32)).astype(BF16)
        return carry

    lax.fori_loop(0, 16, weights, 0)

    take(cb.at[pl.ds(0, 31)], cb_r.at[0])
    collse = lse0(cb[...])[0]
    mp[...] = collse
    new_row = mp[pl.ds(t >> 2, 1), :]
    factor = jnp.exp2(log_target + jnp.concatenate(tops, axis=0) - collse)
    lead = lax.broadcasted_iota(jnp.int32, (16, 128), 0)
    for b in range(4):
        lanes = slice(b * 128, (b + 1) * 128)
        f = factor[b : b + 1, :]
        scaled = yt[:, lanes] * f
        hi = scaled.astype(BF16)
        fs[0:128, lanes] = hi
        fs[144:272, lanes] = (scaled - hi.astype(F32)).astype(BF16)
        top = f.astype(BF16).astype(F32)
        fs[128:144, lanes] = jnp.where(lead == 0, top, jnp.where(lead == 1, f - top, 0.0)).astype(BF16)

    for a in (2, 1, 3, 0):
        quad = (x + a) & 3
        first = jnp.dot(fs[...], eh[pl.ds(quad, 1)][0], preferred_element_type=F32)
        second = jnp.dot(fs[0:144, :], el[pl.ds(quad, 1)][0], preferred_element_type=F32)
        n = first[0:128] + first[144:272] + second[0:128]
        total = first[128:129] + first[129:130] + second[128:129]
        n = jnp.concatenate([n[:, 0:128].T, n[:, 128:256].T], axis=0)
        for h in range(4):
            lanes = slice((h // 2) * 128, (h // 2) * 128 + 128)
            part = jnp.concatenate([n[h * ROWS : (h + 1) * ROWS], total[:, lanes], new_row], axis=0)
            mm[pl.ds(quad * 4 + h, 1)] = part[None]
    for a in (2, 1, 3, 0):
        for b in (2, 1, 3, 0):
            if a or b:
                p = peer(a, b)
                remote(mm.at[p], mb.at[q], mb_s.at[0], mb_r.at[x], plane_device(p)).start()

    mb[pl.ds(q, 1)] = mm[pl.ds(q, 1)]
    total = jnp.zeros((ROWS + 1, 128), F32)
    for a in (0, 1, 3, 2):
        quad = (x + a) & 3
        take(mb.at[pl.ds(0, 4 if a else 3)], mb_r.at[quad])
        got = mb[pl.ds(quad * 4, 4), 0 : ROWS + 1]
        total = total + ((got[0] + got[1]) + (got[2] + got[3]))
    wt[...] = jnp.broadcast_to(1.0 / total[ROWS : ROWS + 1], (128, 128)).T
    out_m[...] = total[0:ROWS] * wt[pl.ds(pl.multiple_of((q & 1) * ROWS, ROWS), ROWS), :]

    new = gather_lanes(mb[:, ROWS + 1 : ROWS + 2].reshape(16, 128), t & 3)
    out_t[...] = gv[...] + 0.5 * (lv[...] - LN2 * new)

    left(tb.at[pl.ds(0, 15)], tb_s.at[0])
    left(xs.at[pl.ds(0, 15)], xs_s.at[0])
    left(rb.at[pl.ds(0, 15)], rb_s.at[0])
    left(cb.at[pl.ds(0, 31)], cb_s.at[0])
    left(mm.at[pl.ds(0, 15)], mb_s.at[0])


def finish(f_ref, t_ref, m_ref, out_f, out_t, out_m):
    out_f[...] = f_ref[...]
    out_t[...] = t_ref[...]
    out_m[...] = m_ref[...]


def shards(points_src, points_tgt, log_source, log_target, target_potential):
    vmem = pl.BlockSpec(memory_space=pltpu.VMEM)
    hbm = pl.BlockSpec(memory_space=pltpu.HBM)
    dma = pltpu.SemaphoreType.DMA
    shapes = (
        jax.ShapeDtypeStruct((1, ROWS), F32),
        jax.ShapeDtypeStruct((4, 128), F32),
        jax.ShapeDtypeStruct((ROWS, 128), F32),
    )
    results = pl.pallas_call(
        kernel,
        name="sinkhorn",
        out_shape=shapes,
        in_specs=[hbm] * 5,
        out_specs=(vmem,) * 3,
        scratch_shapes=[
            pltpu.VMEM((16, ROWS, 128), F32),
            pltpu.VMEM((16, SLICE + 2, 128), F32),
            pltpu.VMEM((4, 128), F32),
            pltpu.VMEM((4, 128), F32),
            pltpu.VMEM((1, ROWS), F32),
            pltpu.VMEM((512, 256), BF16),
            pltpu.VMEM((512, 256), BF16),
            pltpu.VMEM((512, 128), F32),
            pltpu.VMEM((128, 512), F32),
            pltpu.VMEM((512, 128), F32),
            pltpu.VMEM((4, 512, QUAD), F32),
            pltpu.VMEM((4, 512, QUAD), BF16),
            pltpu.VMEM((4, 512, QUAD), BF16),
            pltpu.VMEM((272, 512), BF16),
            pltpu.VMEM((16, 9, 128), F32),
            pltpu.VMEM((8, 128), F32),
            pltpu.VMEM((8, 128), F32),
            pltpu.VMEM((512, 128), F32),
            pltpu.VMEM((32, 4, 128), F32),
            pltpu.VMEM((4, 128), F32),
            pltpu.VMEM((16, ROWS + 2, 128), F32),
            pltpu.VMEM((16, ROWS + 2, 128), F32),
            pltpu.VMEM((128, 128), F32),
            dma((5,)),
            dma((1,)), dma((7,)),
            dma((1,)), dma((4,)), dma((5,)),
            dma((1,)), dma((1,)),
            dma((1,)), dma((1,)),
            dma((1,)), dma((4,)),
        ],
        compiler_params=pltpu.CompilerParams(
            collective_id=0, has_side_effects=True, vmem_limit_bytes=56 * 2**20
        ),
    )(
        points_src,
        points_tgt,
        log_source.reshape(1, ROWS),
        log_target.reshape(4, 128),
        target_potential.reshape(4, 128),
    )
    source_potential, target_new, mapped = pl.pallas_call(
        finish, name="finish", out_shape=shapes, in_specs=[vmem] * 3, out_specs=(vmem,) * 3
    )(*results)
    return source_potential.reshape(ROWS), target_new.reshape(512), mapped


def solution(mesh):
    return jax.shard_map(
        shards,
        mesh=mesh,
        in_specs=(P(("src", "tgt"), None), P("tgt", None), P(("src", "tgt")), P("tgt"), P("tgt")),
        out_specs=(P(("src", "tgt")), P("tgt"), P(("src", "tgt"), None)),
        check_vma=False,
    )
```

```python
import jax
import jax.numpy as jnp
from jax import lax
from jax.experimental import pallas as pl
from jax.experimental.pallas import tpu as pltpu
from jax.sharding import PartitionSpec as P

MESH = pl.DeviceIdType.MESH
F32 = jnp.float32
BF16 = jnp.bfloat16
ROWS = 64
HALF = 32
SLICE = 32
QUAD = 4 * ROWS


def ring(a):
    return min(a, 4 - a)


PEERS = sorted(((a, b) for a in range(4) for b in range(4) if a or b), key=lambda o: -ring(o[0]) - ring(o[1]))

LOG2E = 1.4426950408889634
LN2 = 0.6931471805599453


def lse0(values):
    peak = jnp.max(values, axis=0, keepdims=True)
    return peak + LOG2E * jnp.log(jnp.sum(jnp.exp2(values - peak), axis=0, keepdims=True))


def split3(v):
    hi = v.astype(BF16)
    rest = v - hi.astype(F32)
    mid = rest.astype(BF16)
    return hi, mid, (rest - mid.astype(F32)).astype(BF16)


def gather_lanes(pieces, group):
    lane = lax.broadcasted_iota(jnp.int32, (16, 128), 1) >> 5
    row = lax.broadcasted_iota(jnp.int32, (16, 128), 0) & 3
    whole = jnp.zeros((16, 128), F32)
    for k in range(4):
        turned = pltpu.roll(pieces, ((k - group) & 3) * SLICE, 1)
        whole = whole + jnp.where((lane == k) & (row == k), turned, 0.0)
    return jnp.concatenate([jnp.sum(whole[4 * b : 4 * b + 4], axis=0, keepdims=True) for b in range(4)], axis=0)


def kernel(
    ps, pt, ls, lt, gp,
    out_f, out_t, out_m,
    xs, tb, gv, lv, lsv, y1, y3, yf, yt, aa, sc, eh, el, fs, rb, uu, lsum, cl, cb, mp, mm, mb, wt,
    known, loc, xs_s, xs_r, tb_s, tb_r, fw_r, rb_s, rb_r, cb_s, cb_r, mb_s, mb_r,
):
    s = lax.axis_index("src")
    t = lax.axis_index("tgt")
    q = s >> 1
    zl = t >> 1
    c = t & 1
    z = (s & 1) * 8 + zl
    x = q >> 2
    y = q & 3
    me = z * 2 + c

    def peer(a, b):
        return ((x + a) & 3) * 4 + ((y + b) & 3)

    def plane_device(p):
        return (p * 2 + (s & 1), t)

    def column_device(to_z, to_c):
        return (q * 2 + (to_z >> 3), (to_z & 7) * 2 + to_c)

    def remote(src, dst, send, recv, device):
        return pltpu.make_async_remote_copy(
            src_ref=src, dst_ref=dst, send_sem=send, recv_sem=recv, device_id=device, device_id_type=MESH
        )

    def take(ref, recv):
        remote(ref, ref, recv, recv, plane_device(peer(1, 0))).wait_recv()

    def left(ref, send):
        remote(ref, ref, send, send, plane_device(peer(1, 0))).wait_send()

    barrier = pltpu.get_barrier_semaphore()

    def greet(device, sem=barrier):
        pl.semaphore_signal(sem, inc=1, device_id=device, device_id_type=MESH)

    sibling = column_device(z, 1 - c)
    for k in (2, 1, 3):
        greet(plane_device(peer(k, 0)))
        greet(plane_device(peer(0, k)))
    for d in (2, -2, 1, -1):
        greet(column_device((z + d) & 15, c))
    greet(sibling)

    local = [
        pltpu.make_async_copy(gp, gv, loc.at[0]),
        pltpu.make_async_copy(lt, lv, loc.at[1]),
        pltpu.make_async_copy(pt.at[pl.ds(pl.multiple_of(q * SLICE, SLICE), SLICE)], tb.at[t, pl.ds(0, SLICE)], loc.at[2]),
        pltpu.make_async_copy(ps, xs.at[q], loc.at[3]),
        pltpu.make_async_copy(ls, lsv, loc.at[4]),
    ]
    for copy in local:
        copy.start()
    for copy in local:
        copy.wait()
    tb[pl.ds(t, 1), SLICE : SLICE + 1] = gv[pl.ds(q >> 2, 1), :][None]
    tb[pl.ds(t, 1), SLICE + 1 : SLICE + 2] = lv[pl.ds(q >> 2, 1), :][None]

    pl.semaphore_wait(barrier, 6 + 4 + 1)

    def send_targets(slot, recv, device):
        remote(tb.at[slot], tb.at[slot], tb_s.at[0], recv, device).start()

    def send_half(p, h, recv, to):
        part = xs.at[p, pl.ds(h * HALF, HALF)]
        remote(part, part, xs_s.at[0], recv, plane_device(to)).start()

    def pass_on(p, h):
        for k in (2, 1, 3):
            send_half(p, h, xs_r.at[0], peer(k, 0) if h else peer(0, k))

    def column_slot(off, core):
        return ((zl + off) & 7) * 2 + core

    for k in (2, 1, 3):
        send_half(q, 0, xs_r.at[k], peer(k, 0))
        send_half(q, 1, xs_r.at[3 + k], peer(0, k))
    send_targets(t, tb_r.at[1], column_device((z + 2) & 15, c))
    send_targets(t, tb_r.at[2], column_device((z - 2) & 15, c))
    pass_on(q, 0)
    pass_on(q, 1)
    for d in (1, -1):
        send_targets(t, tb_r.at[0], column_device((z + d) & 15, c))
    send_targets(t, fw_r.at[0], sibling)
    half_block = xs.at[0, pl.ds(0, HALF)]

    def relay_points(k):
        take(half_block, xs_r.at[k])
        pass_on(peer(-k, 0), 0)
        take(half_block, xs_r.at[3 + k])
        pass_on(peer(0, -k), 1)

    relay_points(1)
    take(tb.at[pl.ds(0, 2)], tb_r.at[0])
    take(tb.at[0], tb_r.at[1])
    take(tb.at[0], tb_r.at[2])
    turn = 2 - 4 * c
    for core in range(2):
        send_targets(column_slot(-turn, c), tb_r.at[4], column_device((z + turn) & 15, core))
    for sign in (1, -1):
        for core in range(2):
            send_targets(column_slot(-2 * sign, c), tb_r.at[3], column_device((z + sign) & 15, core))
    relay_points(3)
    relay_points(2)
    for d in (1, 2):
        for off in (d, 8 - d):
            send_targets(column_slot(off, c), fw_r.at[d], sibling)

    lane = lax.broadcasted_iota(jnp.int32, (SLICE, 128), 1)
    sub = lax.broadcasted_iota(jnp.int32, (SLICE, 128), 0)
    mine = lane == sub + (q & 3) * SLICE

    def use_targets(slot):
        block = tb[pl.ds(slot, 1)][0]
        pts = block[0:SLICE]
        rows = pl.ds(pl.multiple_of(slot * SLICE, SLICE), SLICE)
        own = jnp.where(mine, 2.0 * block[SLICE : SLICE + 1], 0.0)
        a = LOG2E * jnp.sum(own - pts * pts, axis=1, keepdims=True)
        aa[rows, :] = jnp.broadcast_to(a, (SLICE, 128))
        hi, mid, lo = split3((2.0 * LOG2E) * pts)
        yf[rows, :] = pts
        y1[rows, 0:128] = hi
        y1[rows, 128:256] = mid
        y3[rows, 0:128] = hi
        y3[rows, 128:256] = lo

    groups = (
        (fw_r.at[0], 1, (0,)),
        (fw_r.at[1], 2, (1, 7)),
        (fw_r.at[2], 2, (2, 6)),
        (tb_r.at[4], 2, (4,)),
        (tb_r.at[3], 4, (3, 5)),
    )
    for sem, count, offsets in groups:
        take(tb.at[pl.ds(0, count)], sem)
        for off in offsets:
            for core in range(2):
                use_targets(column_slot(off, core))
    for d in (2, -2):
        for core in range(2):
            greet(column_device((z + d) & 15, core), known)

    def product(targets, first, second):
        return lax.dot_general(
            targets, jnp.concatenate([first, second], axis=1),
            (((1,), (1,)), ((), ())), preferred_element_type=F32,
        )

    take(xs.at[pl.ds(0, 12)], xs_r.at[0])
    for quad in range(4):
        hi, mid, lo = split3(xs[quad * 4 : quad * 4 + 4].reshape(QUAD, 128))
        prod = product(y3[...], lo, hi) + product(y1[...], mid, hi) + product(y1[...], hi, mid)
        score = prod + jnp.concatenate([aa[...], aa[...]], axis=1)
        sc[quad] = score
        row = lse0(score)
        rb[pl.ds(q, 1), 2 * quad : 2 * quad + 1] = row[:, 0:128][None]
        rb[pl.ds(q, 1), 2 * quad + 1 : 2 * quad + 2] = row[:, 128:256][None]

    half = (lax.broadcasted_iota(jnp.int32, (1, 128), 1) >> 6) == (q & 1)
    both = jnp.concatenate([lsv[...], lsv[...]], axis=1)
    rb[pl.ds(q, 1), 8:9] = jnp.where(half, both, 0.0)[None]
    for a, b in PEERS:
        remote(rb.at[q], rb.at[q], rb_s.at[0], rb_r.at[0], plane_device(peer(a, b))).start()

    for b in range(4):
        yt[:, b * 128 : (b + 1) * 128] = yf[b * 128 : (b + 1) * 128, :].T
    log_target = LOG2E * gather_lanes(tb[:, SLICE + 1 : SLICE + 2].reshape(16, 128), q & 3)
    own_points = xs[pl.ds(q, 1)][0]
    squares = jnp.concatenate([own_points * own_points, jnp.zeros((128 - ROWS, 128), F32)], axis=0)
    norm = jnp.sum(squares.T, axis=0, keepdims=True)

    take(rb.at[pl.ds(0, 15)], rb_r.at[0])
    rowlse = lse0(rb[:, 0:8])[0]
    uu[...] = rowlse
    for b in range(8):
        lsum[b : b + 1, :] = rb[2 * b, 8:9] + rb[2 * b + 1, 8:9]
    u = LOG2E * lsum[...] - rowlse

    def columns(j, carry):
        rows = pl.ds(pl.multiple_of(j * 32, 32), 32)
        vals = []
        for b in range(8):
            lanes = slice((b % 2) * 128, (b % 2) * 128 + 128)
            v = u[b : b + 1, :] + sc[b // 2, rows, lanes]
            sc[b // 2, rows, lanes] = v
            vals.append(v)
        peak = vals[0]
        for v in vals[1:]:
            peak = jnp.maximum(peak, v)
        total = jnp.exp2(vals[0] - peak)
        for v in vals[1:]:
            total = total + jnp.exp2(v - peak)
        cl[rows, :] = peak + LOG2E * jnp.log(total)
        return carry

    lax.fori_loop(0, 16, columns, 0, unroll=True)
    tops = []
    for b in range(4):
        turned = cl[b * 128 : (b + 1) * 128, :].T
        tops.append(jnp.max(turned, axis=0, keepdims=True))
        cb[pl.ds(me, 1), b : b + 1] = lse0(turned)[None]

    pl.semaphore_wait(known, 4)

    def send_columns(d, to_c):
        remote(cb.at[me], cb.at[me], cb_s.at[0], cb_r.at[0], column_device((z + d) & 15, to_c)).start()

    for d in (8, 7, -7, 6, -6, 5, -5, 4, -4, 3, -3, 2, -2, 1, -1):
        for to_c in range(2):
            send_columns(d, to_c)
    send_columns(0, 1 - c)

    own_lse = uu[pl.ds(q >> 1, 1), :]
    own_lse = jnp.where(q & 1 == 0, own_lse, pltpu.roll(own_lse, 64, 1))
    out_f[...] = 0.5 * (lsv[...] + norm[:, 0:ROWS] - LN2 * own_lse[:, 0:ROWS])

    def weights(j, carry):
        rows = pl.ds(pl.multiple_of(j * 32, 32), 32)
        top = jnp.max(cl[rows, :], axis=1, keepdims=True)
        for quad in range(4):
            w = jnp.exp2(sc[quad, rows, :] - top)
            hi = w.astype(BF16)
            eh[quad, rows, :] = hi
            el[quad, rows, :] = (w - hi.astype(F32)).astype(BF16)
        return carry

    lax.fori_loop(0, 16, weights, 0)

    take(cb.at[pl.ds(0, 31)], cb_r.at[0])
    collse = lse0(cb[...])[0]
    mp[...] = collse
    new_row = mp[pl.ds(t >> 2, 1), :]
    factor = jnp.exp2(log_target + jnp.concatenate(tops, axis=0) - collse)
    lead = lax.broadcasted_iota(jnp.int32, (16, 128), 0)
    for b in range(4):
        lanes = slice(b * 128, (b + 1) * 128)
        f = factor[b : b + 1, :]
        scaled = yt[:, lanes] * f
        hi = scaled.astype(BF16)
        fs[0:128, lanes] = hi
        fs[144:272, lanes] = (scaled - hi.astype(F32)).astype(BF16)
        top = f.astype(BF16).astype(F32)
        fs[128:144, lanes] = jnp.where(lead == 0, top, jnp.where(lead == 1, f - top, 0.0)).astype(BF16)

    for a in (2, 1, 3, 0):
        quad = (x + a) & 3
        first = jnp.dot(fs[...], eh[pl.ds(quad, 1)][0], preferred_element_type=F32)
        second = jnp.dot(fs[0:144, :], el[pl.ds(quad, 1)][0], preferred_element_type=F32)
        n = first[0:128] + first[144:272] + second[0:128]
        total = first[128:129] + first[129:130] + second[128:129]
        n = jnp.concatenate([n[:, 0:128].T, n[:, 128:256].T], axis=0)
        for h in range(4):
            lanes = slice((h // 2) * 128, (h // 2) * 128 + 128)
            part = jnp.concatenate([n[h * ROWS : (h + 1) * ROWS], total[:, lanes], new_row], axis=0)
            mm[pl.ds(quad * 4 + h, 1)] = part[None]
    for a in (2, 1, 3, 0):
        for b in (2, 1, 3, 0):
            if a or b:
                p = peer(a, b)
                remote(mm.at[p], mb.at[q], mb_s.at[0], mb_r.at[x], plane_device(p)).start()

    mb[pl.ds(q, 1)] = mm[pl.ds(q, 1)]
    total = jnp.zeros((ROWS + 1, 128), F32)
    for a in (0, 1, 3, 2):
        quad = (x + a) & 3
        take(mb.at[pl.ds(0, 4 if a else 3)], mb_r.at[quad])
        got = mb[pl.ds(quad * 4, 4), 0 : ROWS + 1]
        total = total + ((got[0] + got[1]) + (got[2] + got[3]))
    wt[...] = jnp.broadcast_to(1.0 / total[ROWS : ROWS + 1], (128, 128)).T
    out_m[...] = total[0:ROWS] * wt[pl.ds(pl.multiple_of((q & 1) * ROWS, ROWS), ROWS), :]

    new = gather_lanes(mb[:, ROWS + 1 : ROWS + 2].reshape(16, 128), t & 3)
    out_t[...] = gv[...] + 0.5 * (lv[...] - LN2 * new)

    left(tb.at[pl.ds(0, 15)], tb_s.at[0])
    left(xs.at[pl.ds(0, 15)], xs_s.at[0])
    left(rb.at[pl.ds(0, 15)], rb_s.at[0])
    left(cb.at[pl.ds(0, 31)], cb_s.at[0])
    left(mm.at[pl.ds(0, 15)], mb_s.at[0])


def finish(f_ref, t_ref, m_ref, out_f, out_t, out_m):
    out_f[...] = f_ref[...]
    out_t[...] = t_ref[...]
    out_m[...] = m_ref[...]


def shards(points_src, points_tgt, log_source, log_target, target_potential):
    vmem = pl.BlockSpec(memory_space=pltpu.VMEM)
    hbm = pl.BlockSpec(memory_space=pltpu.HBM)
    dma = pltpu.SemaphoreType.DMA
    shapes = (
        jax.ShapeDtypeStruct((1, ROWS), F32),
        jax.ShapeDtypeStruct((4, 128), F32),
        jax.ShapeDtypeStruct((ROWS, 128), F32),
    )
    results = pl.pallas_call(
        kernel,
        name="sinkhorn",
        out_shape=tuple(pltpu.VMEM(v.shape, v.dtype) for v in shapes),
        in_specs=[hbm] * 5,
        out_specs=(vmem,) * 3,
        scratch_shapes=[
            pltpu.VMEM((16, ROWS, 128), F32),
            pltpu.VMEM((16, SLICE + 2, 128), F32),
            pltpu.VMEM((4, 128), F32),
            pltpu.VMEM((4, 128), F32),
            pltpu.VMEM((1, ROWS), F32),
            pltpu.VMEM((512, 256), BF16),
            pltpu.VMEM((512, 256), BF16),
            pltpu.VMEM((512, 128), F32),
            pltpu.VMEM((128, 512), F32),
            pltpu.VMEM((512, 128), F32),
            pltpu.VMEM((4, 512, QUAD), F32),
            pltpu.VMEM((4, 512, QUAD), BF16),
            pltpu.VMEM((4, 512, QUAD), BF16),
            pltpu.VMEM((272, 512), BF16),
            pltpu.VMEM((16, 9, 128), F32),
            pltpu.VMEM((8, 128), F32),
            pltpu.VMEM((8, 128), F32),
            pltpu.VMEM((512, 128), F32),
            pltpu.VMEM((32, 4, 128), F32),
            pltpu.VMEM((4, 128), F32),
            pltpu.VMEM((16, ROWS + 2, 128), F32),
            pltpu.VMEM((16, ROWS + 2, 128), F32),
            pltpu.VMEM((128, 128), F32),
            pltpu.SemaphoreType.REGULAR,
            dma((5,)),
            dma((1,)), dma((7,)),
            dma((1,)), dma((5,)), dma((3,)),
            dma((1,)), dma((1,)),
            dma((1,)), dma((1,)),
            dma((1,)), dma((4,)),
        ],
        compiler_params=pltpu.CompilerParams(
            collective_id=0, has_side_effects=True, vmem_limit_bytes=40 * 2**20
        ),
    )(
        *(
            pltpu.with_memory_space_constraint(v, pltpu.HBM)
            for v in (
                points_src,
                points_tgt,
                log_source.reshape(1, ROWS),
                log_target.reshape(4, 128),
                target_potential.reshape(4, 128),
            )
        )
    )
    source_potential, target_new, mapped = pl.pallas_call(
        finish, name="finish", out_shape=shapes, in_specs=[vmem] * 3, out_specs=(vmem,) * 3
    )(*(pltpu.with_memory_space_constraint(v, pltpu.VMEM) for v in results))
    return source_potential.reshape(ROWS), target_new.reshape(512), mapped


def solution(mesh):
    return jax.shard_map(
        shards,
        mesh=mesh,
        in_specs=(P(("src", "tgt"), None), P("tgt", None), P(("src", "tgt")), P("tgt"), P("tgt")),
        out_specs=(P(("src", "tgt")), P("tgt"), P(("src", "tgt"), None)),
        check_vma=False,
    )
```

```python
import jax
import jax.numpy as jnp
from jax import lax
from jax.experimental import pallas as pl
from jax.experimental.pallas import tpu as pltpu
from jax.sharding import PartitionSpec as P

MESH = pl.DeviceIdType.MESH
F32 = jnp.float32
BF16 = jnp.bfloat16
ROWS = 64
HALF = 32
SLICE = 32
QUAD = 4 * ROWS


def ring(a):
    return min(a, 4 - a)


PEERS = sorted(((a, b) for a in range(4) for b in range(4) if a or b), key=lambda o: -ring(o[0]) - ring(o[1]))

LOG2E = 1.4426950408889634
LN2 = 0.6931471805599453


def lse0(values):
    peak = jnp.max(values, axis=0, keepdims=True)
    return peak + LOG2E * jnp.log(jnp.sum(jnp.exp2(values - peak), axis=0, keepdims=True))


def split3(v):
    hi = v.astype(BF16)
    rest = v - hi.astype(F32)
    mid = rest.astype(BF16)
    return hi, mid, (rest - mid.astype(F32)).astype(BF16)


def gather_lanes(pieces, group):
    lane = lax.broadcasted_iota(jnp.int32, (16, 128), 1) >> 5
    row = lax.broadcasted_iota(jnp.int32, (16, 128), 0) & 3
    whole = jnp.zeros((16, 128), F32)
    for k in range(4):
        turned = pltpu.roll(pieces, ((k - group) & 3) * SLICE, 1)
        whole = whole + jnp.where((lane == k) & (row == k), turned, 0.0)
    return jnp.concatenate([jnp.sum(whole[4 * b : 4 * b + 4], axis=0, keepdims=True) for b in range(4)], axis=0)


def kernel(
    ps, pt, ls, lt, gp,
    out_f, out_t, out_m,
    xs, tb, gv, lv, lsv, y1, y3, yf, yt, aa, sc, eh, el, fs, rb, uu, lsum, cl, cb, mp, mm, mb, wt,
    known, loc, xs_s, xs_r, tb_s, tb_r, fw_r, rb_s, rb_r, cb_s, cb_r, mb_s, mb_r,
):
    s = lax.axis_index("src")
    t = lax.axis_index("tgt")
    q = s >> 1
    zl = t >> 1
    c = t & 1
    z = (s & 1) * 8 + zl
    x = q >> 2
    y = q & 3
    me = z * 2 + c

    def peer(a, b):
        return ((x + a) & 3) * 4 + ((y + b) & 3)

    def plane_device(p):
        return (p * 2 + (s & 1), t)

    def column_device(to_z, to_c):
        return (q * 2 + (to_z >> 3), (to_z & 7) * 2 + to_c)

    def remote(src, dst, send, recv, device):
        return pltpu.make_async_remote_copy(
            src_ref=src, dst_ref=dst, send_sem=send, recv_sem=recv, device_id=device, device_id_type=MESH
        )

    def take(ref, recv):
        remote(ref, ref, recv, recv, plane_device(peer(1, 0))).wait_recv()

    def left(ref, send):
        remote(ref, ref, send, send, plane_device(peer(1, 0))).wait_send()

    barrier = pltpu.get_barrier_semaphore()

    def greet(device, sem=barrier):
        pl.semaphore_signal(sem, inc=1, device_id=device, device_id_type=MESH)

    sibling = column_device(z, 1 - c)
    for k in (2, 1, 3):
        greet(plane_device(peer(k, 0)))
        greet(plane_device(peer(0, k)))
    for d in (2, -2, 1, -1):
        greet(column_device((z + d) & 15, c))
    greet(sibling)

    local = [
        pltpu.make_async_copy(gp, gv, loc.at[0]),
        pltpu.make_async_copy(lt, lv, loc.at[1]),
        pltpu.make_async_copy(pt.at[pl.ds(pl.multiple_of(q * SLICE, SLICE), SLICE)], tb.at[t, pl.ds(0, SLICE)], loc.at[2]),
        pltpu.make_async_copy(ps, xs.at[q], loc.at[3]),
        pltpu.make_async_copy(ls, lsv, loc.at[4]),
    ]
    for copy in local:
        copy.start()
    for copy in local:
        copy.wait()
    tb[pl.ds(t, 1), SLICE : SLICE + 1] = gv[pl.ds(q >> 2, 1), :][None]
    tb[pl.ds(t, 1), SLICE + 1 : SLICE + 2] = lv[pl.ds(q >> 2, 1), :][None]

    pl.semaphore_wait(barrier, 6 + 4 + 1)

    def send_targets(slot, recv, device):
        remote(tb.at[slot], tb.at[slot], tb_s.at[0], recv, device).start()

    def send_half(p, h, recv, to):
        part = xs.at[p, pl.ds(h * HALF, HALF)]
        remote(part, part, xs_s.at[0], recv, plane_device(to)).start()

    def pass_on(p, h):
        for k in (2, 1, 3):
            send_half(p, h, xs_r.at[0], peer(k, 0) if h else peer(0, k))

    def column_slot(off, core):
        return ((zl + off) & 7) * 2 + core

    send_targets(t, tb_r.at[1], column_device((z + 2) & 15, c))
    send_targets(t, tb_r.at[2], column_device((z - 2) & 15, c))
    for k in (1, 3, 2):
        send_half(q, 0, xs_r.at[k], peer(k, 0))
        send_half(q, 1, xs_r.at[3 + k], peer(0, k))
    for d in (1, -1):
        send_targets(t, tb_r.at[0], column_device((z + d) & 15, c))
    pass_on(q, 0)
    pass_on(q, 1)
    send_targets(t, fw_r.at[0], sibling)
    half_block = xs.at[0, pl.ds(0, HALF)]

    def relay_points(k):
        take(half_block, xs_r.at[k])
        pass_on(peer(-k, 0), 0)
        take(half_block, xs_r.at[3 + k])
        pass_on(peer(0, -k), 1)

    relay_points(1)
    take(tb.at[pl.ds(0, 2)], tb_r.at[0])
    take(tb.at[0], tb_r.at[1])
    take(tb.at[0], tb_r.at[2])
    turn = 2 - 4 * c
    for core in range(2):
        send_targets(column_slot(-turn, c), tb_r.at[4], column_device((z + turn) & 15, core))
    for sign in (1, -1):
        for core in range(2):
            send_targets(column_slot(-2 * sign, c), tb_r.at[3], column_device((z + sign) & 15, core))
    relay_points(3)
    relay_points(2)
    for d in (1, 2):
        for off in (d, 8 - d):
            send_targets(column_slot(off, c), fw_r.at[d], sibling)

    lane = lax.broadcasted_iota(jnp.int32, (SLICE, 128), 1)
    sub = lax.broadcasted_iota(jnp.int32, (SLICE, 128), 0)
    mine = lane == sub + (q & 3) * SLICE

    def use_targets(slot):
        block = tb[pl.ds(slot, 1)][0]
        pts = block[0:SLICE]
        rows = pl.ds(pl.multiple_of(slot * SLICE, SLICE), SLICE)
        own = jnp.where(mine, 2.0 * block[SLICE : SLICE + 1], 0.0)
        a = LOG2E * jnp.sum(own - pts * pts, axis=1, keepdims=True)
        aa[rows, :] = jnp.broadcast_to(a, (SLICE, 128))
        hi, mid, lo = split3((2.0 * LOG2E) * pts)
        yf[rows, :] = pts
        y1[rows, 0:128] = hi
        y1[rows, 128:256] = mid
        y3[rows, 0:128] = hi
        y3[rows, 128:256] = lo

    groups = (
        (fw_r.at[0], 1, (0,)),
        (fw_r.at[1], 2, (1, 7)),
        (fw_r.at[2], 2, (2, 6)),
        (tb_r.at[4], 2, (4,)),
        (tb_r.at[3], 4, (3, 5)),
    )
    for sem, count, offsets in groups:
        take(tb.at[pl.ds(0, count)], sem)
        for off in offsets:
            for core in range(2):
                use_targets(column_slot(off, core))
    for d in (2, -2):
        for core in range(2):
            greet(column_device((z + d) & 15, core), known)

    def product(targets, first, second):
        return lax.dot_general(
            targets, jnp.concatenate([first, second], axis=1),
            (((1,), (1,)), ((), ())), preferred_element_type=F32,
        )

    take(xs.at[pl.ds(0, 12)], xs_r.at[0])
    for quad in range(4):
        hi, mid, lo = split3(xs[quad * 4 : quad * 4 + 4].reshape(QUAD, 128))
        prod = product(y3[...], lo, hi) + product(y1[...], mid, hi) + product(y1[...], hi, mid)
        score = prod + jnp.concatenate([aa[...], aa[...]], axis=1)
        sc[quad] = score
        row = lse0(score)
        rb[pl.ds(q, 1), 2 * quad : 2 * quad + 1] = row[:, 0:128][None]
        rb[pl.ds(q, 1), 2 * quad + 1 : 2 * quad + 2] = row[:, 128:256][None]

    half = (lax.broadcasted_iota(jnp.int32, (1, 128), 1) >> 6) == (q & 1)
    both = jnp.concatenate([lsv[...], lsv[...]], axis=1)
    rb[pl.ds(q, 1), 8:9] = jnp.where(half, both, 0.0)[None]
    for a, b in PEERS:
        remote(rb.at[q], rb.at[q], rb_s.at[0], rb_r.at[0], plane_device(peer(a, b))).start()

    for b in range(4):
        yt[:, b * 128 : (b + 1) * 128] = yf[b * 128 : (b + 1) * 128, :].T
    log_target = LOG2E * gather_lanes(tb[:, SLICE + 1 : SLICE + 2].reshape(16, 128), q & 3)
    own_points = xs[pl.ds(q, 1)][0]
    squares = jnp.concatenate([own_points * own_points, jnp.zeros((128 - ROWS, 128), F32)], axis=0)
    norm = jnp.sum(squares.T, axis=0, keepdims=True)

    take(rb.at[pl.ds(0, 15)], rb_r.at[0])
    rowlse = lse0(rb[:, 0:8])[0]
    uu[...] = rowlse
    for b in range(8):
        lsum[b : b + 1, :] = rb[2 * b, 8:9] + rb[2 * b + 1, 8:9]
    u = LOG2E * lsum[...] - rowlse

    def columns(j, carry):
        rows = pl.ds(pl.multiple_of(j * 32, 32), 32)
        vals = []
        for b in range(8):
            lanes = slice((b % 2) * 128, (b % 2) * 128 + 128)
            v = u[b : b + 1, :] + sc[b // 2, rows, lanes]
            sc[b // 2, rows, lanes] = v
            vals.append(v)
        peak = vals[0]
        for v in vals[1:]:
            peak = jnp.maximum(peak, v)
        total = jnp.exp2(vals[0] - peak)
        for v in vals[1:]:
            total = total + jnp.exp2(v - peak)
        cl[rows, :] = peak + LOG2E * jnp.log(total)
        return carry

    lax.fori_loop(0, 16, columns, 0, unroll=True)
    tops = []
    for b in range(4):
        turned = cl[b * 128 : (b + 1) * 128, :].T
        tops.append(jnp.max(turned, axis=0, keepdims=True))
        cb[pl.ds(me, 1), b : b + 1] = lse0(turned)[None]

    pl.semaphore_wait(known, 4)

    def send_columns(d, to_c):
        remote(cb.at[me], cb.at[me], cb_s.at[0], cb_r.at[0], column_device((z + d) & 15, to_c)).start()

    for d in (8, 7, -7, 6, -6, 5, -5, 4, -4, 3, -3, 2, -2, 1, -1):
        for to_c in range(2):
            send_columns(d, to_c)
    send_columns(0, 1 - c)

    own_lse = uu[pl.ds(q >> 1, 1), :]
    own_lse = jnp.where(q & 1 == 0, own_lse, pltpu.roll(own_lse, 64, 1))
    out_f[...] = 0.5 * (lsv[...] + norm[:, 0:ROWS] - LN2 * own_lse[:, 0:ROWS])

    def weights(j, carry):
        rows = pl.ds(pl.multiple_of(j * 32, 32), 32)
        top = jnp.max(cl[rows, :], axis=1, keepdims=True)
        for quad in range(4):
            w = jnp.exp2(sc[quad, rows, :] - top)
            hi = w.astype(BF16)
            eh[quad, rows, :] = hi
            el[quad, rows, :] = (w - hi.astype(F32)).astype(BF16)
        return carry

    lax.fori_loop(0, 16, weights, 0)

    take(cb.at[pl.ds(0, 31)], cb_r.at[0])
    collse = lse0(cb[...])[0]
    mp[...] = collse
    new_row = mp[pl.ds(t >> 2, 1), :]
    factor = jnp.exp2(log_target + jnp.concatenate(tops, axis=0) - collse)
    lead = lax.broadcasted_iota(jnp.int32, (16, 128), 0)
    for b in range(4):
        lanes = slice(b * 128, (b + 1) * 128)
        f = factor[b : b + 1, :]
        scaled = yt[:, lanes] * f
        hi = scaled.astype(BF16)
        fs[0:128, lanes] = hi
        fs[144:272, lanes] = (scaled - hi.astype(F32)).astype(BF16)
        top = f.astype(BF16).astype(F32)
        fs[128:144, lanes] = jnp.where(lead == 0, top, jnp.where(lead == 1, f - top, 0.0)).astype(BF16)

    for a in (2, 1, 3, 0):
        quad = (x + a) & 3
        first = jnp.dot(fs[...], eh[pl.ds(quad, 1)][0], preferred_element_type=F32)
        second = jnp.dot(fs[0:144, :], el[pl.ds(quad, 1)][0], preferred_element_type=F32)
        n = first[0:128] + first[144:272] + second[0:128]
        total = first[128:129] + first[129:130] + second[128:129]
        n = jnp.concatenate([n[:, 0:128].T, n[:, 128:256].T], axis=0)
        for h in range(4):
            lanes = slice((h // 2) * 128, (h // 2) * 128 + 128)
            part = jnp.concatenate([n[h * ROWS : (h + 1) * ROWS], total[:, lanes], new_row], axis=0)
            mm[pl.ds(quad * 4 + h, 1)] = part[None]
    for a in (2, 1, 3, 0):
        for b in (2, 1, 3, 0):
            if a or b:
                p = peer(a, b)
                remote(mm.at[p], mb.at[q], mb_s.at[0], mb_r.at[x], plane_device(p)).start()

    mb[pl.ds(q, 1)] = mm[pl.ds(q, 1)]
    total = jnp.zeros((ROWS + 1, 128), F32)
    for a in range(4):
        take(mb.at[pl.ds(0, 4 if a else 3)], mb_r.at[(x + a) & 3])
    for quad in range(4):
        got = mb[pl.ds(quad * 4, 4), 0 : ROWS + 1]
        total = total + ((got[0] + got[1]) + (got[2] + got[3]))
    wt[...] = jnp.broadcast_to(1.0 / total[ROWS : ROWS + 1], (128, 128)).T
    out_m[...] = total[0:ROWS] * wt[pl.ds(pl.multiple_of((q & 1) * ROWS, ROWS), ROWS), :]

    new = gather_lanes(mb[:, ROWS + 1 : ROWS + 2].reshape(16, 128), t & 3)
    out_t[...] = gv[...] + 0.5 * (lv[...] - LN2 * new)

    left(tb.at[pl.ds(0, 15)], tb_s.at[0])
    left(xs.at[pl.ds(0, 15)], xs_s.at[0])
    left(rb.at[pl.ds(0, 15)], rb_s.at[0])
    left(cb.at[pl.ds(0, 31)], cb_s.at[0])
    left(mm.at[pl.ds(0, 15)], mb_s.at[0])


def finish(f_ref, t_ref, m_ref, out_f, out_t, out_m):
    out_f[...] = f_ref[...]
    out_t[...] = t_ref[...]
    out_m[...] = m_ref[...]


def shards(points_src, points_tgt, log_source, log_target, target_potential):
    vmem = pl.BlockSpec(memory_space=pltpu.VMEM)
    hbm = pl.BlockSpec(memory_space=pltpu.HBM)
    dma = pltpu.SemaphoreType.DMA
    shapes = (
        jax.ShapeDtypeStruct((1, ROWS), F32),
        jax.ShapeDtypeStruct((4, 128), F32),
        jax.ShapeDtypeStruct((ROWS, 128), F32),
    )
    results = pl.pallas_call(
        kernel,
        name="sinkhorn",
        out_shape=tuple(pltpu.VMEM(v.shape, v.dtype) for v in shapes),
        in_specs=[hbm] * 5,
        out_specs=(vmem,) * 3,
        scratch_shapes=[
            pltpu.VMEM((16, ROWS, 128), F32),
            pltpu.VMEM((16, SLICE + 2, 128), F32),
            pltpu.VMEM((4, 128), F32),
            pltpu.VMEM((4, 128), F32),
            pltpu.VMEM((1, ROWS), F32),
            pltpu.VMEM((512, 256), BF16),
            pltpu.VMEM((512, 256), BF16),
            pltpu.VMEM((512, 128), F32),
            pltpu.VMEM((128, 512), F32),
            pltpu.VMEM((512, 128), F32),
            pltpu.VMEM((4, 512, QUAD), F32),
            pltpu.VMEM((4, 512, QUAD), BF16),
            pltpu.VMEM((4, 512, QUAD), BF16),
            pltpu.VMEM((272, 512), BF16),
            pltpu.VMEM((16, 9, 128), F32),
            pltpu.VMEM((8, 128), F32),
            pltpu.VMEM((8, 128), F32),
            pltpu.VMEM((512, 128), F32),
            pltpu.VMEM((32, 4, 128), F32),
            pltpu.VMEM((4, 128), F32),
            pltpu.VMEM((16, ROWS + 2, 128), F32),
            pltpu.VMEM((16, ROWS + 2, 128), F32),
            pltpu.VMEM((128, 128), F32),
            pltpu.SemaphoreType.REGULAR,
            dma((5,)),
            dma((1,)), dma((7,)),
            dma((1,)), dma((5,)), dma((3,)),
            dma((1,)), dma((1,)),
            dma((1,)), dma((1,)),
            dma((1,)), dma((4,)),
        ],
        compiler_params=pltpu.CompilerParams(
            collective_id=0, has_side_effects=True, vmem_limit_bytes=40 * 2**20
        ),
    )(
        *(
            pltpu.with_memory_space_constraint(v, pltpu.HBM)
            for v in (
                points_src,
                points_tgt,
                log_source.reshape(1, ROWS),
                log_target.reshape(4, 128),
                target_potential.reshape(4, 128),
            )
        )
    )
    source_potential, target_new, mapped = pl.pallas_call(
        finish, name="finish", out_shape=shapes, in_specs=[vmem] * 3, out_specs=(vmem,) * 3
    )(*(pltpu.with_memory_space_constraint(v, pltpu.VMEM) for v in results))
    return source_potential.reshape(ROWS), target_new.reshape(512), mapped


def solution(mesh):
    return jax.shard_map(
        shards,
        mesh=mesh,
        in_specs=(P(("src", "tgt"), None), P("tgt", None), P(("src", "tgt")), P("tgt"), P("tgt")),
        out_specs=(P(("src", "tgt")), P("tgt"), P(("src", "tgt"), None)),
        check_vma=False,
    )
```

```python
import jax
import jax.numpy as jnp
from jax import lax
from jax.experimental import pallas as pl
from jax.experimental.pallas import tpu as pltpu
from jax.sharding import PartitionSpec as P

MESH = pl.DeviceIdType.MESH
F32 = jnp.float32
BF16 = jnp.bfloat16
ROWS = 64
HALF = 32
SLICE = 32
QUAD = 4 * ROWS


def ring(a):
    return min(a, 4 - a)


PEERS = sorted(((a, b) for a in range(4) for b in range(4) if a or b), key=lambda o: -ring(o[0]) - ring(o[1]))

LOG2E = 1.4426950408889634
LN2 = 0.6931471805599453


def lse0(values):
    peak = jnp.max(values, axis=0, keepdims=True)
    return peak + LOG2E * jnp.log(jnp.sum(jnp.exp2(values - peak), axis=0, keepdims=True))


def split3(v):
    hi = v.astype(BF16)
    rest = v - hi.astype(F32)
    mid = rest.astype(BF16)
    return hi, mid, (rest - mid.astype(F32)).astype(BF16)


def gather_lanes(pieces, group):
    lane = lax.broadcasted_iota(jnp.int32, (16, 128), 1) >> 5
    row = lax.broadcasted_iota(jnp.int32, (16, 128), 0) & 3
    whole = jnp.zeros((16, 128), F32)
    for k in range(4):
        turned = pltpu.roll(pieces, ((k - group) & 3) * SLICE, 1)
        whole = whole + jnp.where((lane == k) & (row == k), turned, 0.0)
    return jnp.concatenate([jnp.sum(whole[4 * b : 4 * b + 4], axis=0, keepdims=True) for b in range(4)], axis=0)


def kernel(
    ps, pt, ls, lt, gp,
    out_f, out_t, out_m,
    xs, tb, gv, lv, lsv, y1, y3, yf, yt, aa, sc, eh, el, fs, rb, uu, lsum, cl, cb, mp, mm, mb, wt,
    known, loc, xs_s, xs_r, tb_s, tb_r, fw_r, rb_s, rb_r, cb_s, cb_r, mb_s, mb_r,
):
    s = lax.axis_index("src")
    t = lax.axis_index("tgt")
    q = s >> 1
    zl = t >> 1
    c = t & 1
    z = (s & 1) * 8 + zl
    x = q >> 2
    y = q & 3
    me = z * 2 + c

    def peer(a, b):
        return ((x + a) & 3) * 4 + ((y + b) & 3)

    def plane_device(p):
        return (p * 2 + (s & 1), t)

    def column_device(to_z, to_c):
        return (q * 2 + (to_z >> 3), (to_z & 7) * 2 + to_c)

    def remote(src, dst, send, recv, device):
        return pltpu.make_async_remote_copy(
            src_ref=src, dst_ref=dst, send_sem=send, recv_sem=recv, device_id=device, device_id_type=MESH
        )

    def take(ref, recv):
        remote(ref, ref, recv, recv, plane_device(peer(1, 0))).wait_recv()

    def left(ref, send):
        remote(ref, ref, send, send, plane_device(peer(1, 0))).wait_send()

    barrier = pltpu.get_barrier_semaphore()

    def greet(device, sem=barrier):
        pl.semaphore_signal(sem, inc=1, device_id=device, device_id_type=MESH)

    sibling = column_device(z, 1 - c)
    for k in (2, 1, 3):
        greet(plane_device(peer(k, 0)))
        greet(plane_device(peer(0, k)))
    for d in (2, -2, 1, -1):
        greet(column_device((z + d) & 15, c))
    greet(sibling)

    local = [
        pltpu.make_async_copy(gp, gv, loc.at[0]),
        pltpu.make_async_copy(lt, lv, loc.at[1]),
        pltpu.make_async_copy(pt.at[pl.ds(pl.multiple_of(q * SLICE, SLICE), SLICE)], tb.at[t, pl.ds(0, SLICE)], loc.at[2]),
        pltpu.make_async_copy(ps, xs.at[q], loc.at[3]),
        pltpu.make_async_copy(ls, lsv, loc.at[4]),
    ]
    for copy in local:
        copy.start()
    for copy in local[:3]:
        copy.wait()
    tb[pl.ds(t, 1), SLICE : SLICE + 1] = gv[pl.ds(q >> 2, 1), :][None]
    tb[pl.ds(t, 1), SLICE + 1 : SLICE + 2] = lv[pl.ds(q >> 2, 1), :][None]

    pl.semaphore_wait(barrier, 6 + 4 + 1)

    def send_targets(slot, recv, device):
        remote(tb.at[slot], tb.at[slot], tb_s.at[0], recv, device).start()

    def send_half(p, h, recv, to, own=False):
        rows = pl.ds(h * HALF, HALF)
        part = xs.at[p, rows]
        remote(ps.at[rows] if own else part, part, xs_s.at[0], recv, plane_device(to)).start()

    def pass_on(p, h, own=False):
        for k in (2, 1, 3):
            send_half(p, h, xs_r.at[0], peer(k, 0) if h else peer(0, k), own)

    def column_slot(off, core):
        return ((zl + off) & 7) * 2 + core

    send_targets(t, tb_r.at[1], column_device((z + 2) & 15, c))
    send_targets(t, tb_r.at[2], column_device((z - 2) & 15, c))
    for k in (1, 3, 2):
        send_half(q, 0, xs_r.at[k], peer(k, 0), True)
        send_half(q, 1, xs_r.at[3 + k], peer(0, k), True)
    for d in (1, -1):
        send_targets(t, tb_r.at[0], column_device((z + d) & 15, c))
    pass_on(q, 0, True)
    pass_on(q, 1, True)
    send_targets(t, fw_r.at[0], sibling)
    half_block = xs.at[0, pl.ds(0, HALF)]

    def relay_points(k):
        take(half_block, xs_r.at[k])
        pass_on(peer(-k, 0), 0)
        take(half_block, xs_r.at[3 + k])
        pass_on(peer(0, -k), 1)

    relay_points(1)
    take(tb.at[pl.ds(0, 2)], tb_r.at[0])
    take(tb.at[0], tb_r.at[1])
    take(tb.at[0], tb_r.at[2])
    turn = 2 - 4 * c
    for core in range(2):
        send_targets(column_slot(-turn, c), tb_r.at[4], column_device((z + turn) & 15, core))
    for sign in (1, -1):
        for core in range(2):
            send_targets(column_slot(-2 * sign, c), tb_r.at[3], column_device((z + sign) & 15, core))
    relay_points(3)
    relay_points(2)
    for d in (1, 2):
        for off in (d, 8 - d):
            send_targets(column_slot(off, c), fw_r.at[d], sibling)

    lane = lax.broadcasted_iota(jnp.int32, (SLICE, 128), 1)
    sub = lax.broadcasted_iota(jnp.int32, (SLICE, 128), 0)
    mine = lane == sub + (q & 3) * SLICE

    def use_targets(slot):
        block = tb[pl.ds(slot, 1)][0]
        pts = block[0:SLICE]
        rows = pl.ds(pl.multiple_of(slot * SLICE, SLICE), SLICE)
        own = jnp.where(mine, 2.0 * block[SLICE : SLICE + 1], 0.0)
        a = LOG2E * jnp.sum(own - pts * pts, axis=1, keepdims=True)
        aa[rows, :] = jnp.broadcast_to(a, (SLICE, 128))
        hi, mid, lo = split3((2.0 * LOG2E) * pts)
        yf[rows, :] = pts
        y1[rows, 0:128] = hi
        y1[rows, 128:256] = mid
        y3[rows, 0:128] = hi
        y3[rows, 128:256] = lo

    groups = (
        (fw_r.at[0], 1, (0,)),
        (fw_r.at[1], 2, (1, 7)),
        (fw_r.at[2], 2, (2, 6)),
        (tb_r.at[4], 2, (4,)),
        (tb_r.at[3], 4, (3, 5)),
    )
    for sem, count, offsets in groups:
        take(tb.at[pl.ds(0, count)], sem)
        for off in offsets:
            for core in range(2):
                use_targets(column_slot(off, core))
    for d in (2, -2):
        for core in range(2):
            greet(column_device((z + d) & 15, core), known)

    def product(targets, first, second):
        return lax.dot_general(
            targets, jnp.concatenate([first, second], axis=1),
            (((1,), (1,)), ((), ())), preferred_element_type=F32,
        )

    for copy in local[3:]:
        copy.wait()
    take(xs.at[pl.ds(0, 12)], xs_r.at[0])
    for quad in range(4):
        hi, mid, lo = split3(xs[quad * 4 : quad * 4 + 4].reshape(QUAD, 128))
        prod = product(y3[...], lo, hi) + product(y1[...], mid, hi) + product(y1[...], hi, mid)
        score = prod + jnp.concatenate([aa[...], aa[...]], axis=1)
        sc[quad] = score
        row = lse0(score)
        rb[pl.ds(q, 1), 2 * quad : 2 * quad + 1] = row[:, 0:128][None]
        rb[pl.ds(q, 1), 2 * quad + 1 : 2 * quad + 2] = row[:, 128:256][None]

    half = (lax.broadcasted_iota(jnp.int32, (1, 128), 1) >> 6) == (q & 1)
    both = jnp.concatenate([lsv[...], lsv[...]], axis=1)
    rb[pl.ds(q, 1), 8:9] = jnp.where(half, both, 0.0)[None]
    for a, b in PEERS:
        remote(rb.at[q], rb.at[q], rb_s.at[0], rb_r.at[0], plane_device(peer(a, b))).start()

    for b in range(4):
        yt[:, b * 128 : (b + 1) * 128] = yf[b * 128 : (b + 1) * 128, :].T
    log_target = LOG2E * gather_lanes(tb[:, SLICE + 1 : SLICE + 2].reshape(16, 128), q & 3)
    own_points = xs[pl.ds(q, 1)][0]
    squares = jnp.concatenate([own_points * own_points, jnp.zeros((128 - ROWS, 128), F32)], axis=0)
    norm = jnp.sum(squares.T, axis=0, keepdims=True)

    take(rb.at[pl.ds(0, 15)], rb_r.at[0])
    rowlse = lse0(rb[:, 0:8])[0]
    uu[...] = rowlse
    for b in range(8):
        lsum[b : b + 1, :] = rb[2 * b, 8:9] + rb[2 * b + 1, 8:9]
    u = LOG2E * lsum[...] - rowlse

    def columns(j, carry):
        rows = pl.ds(pl.multiple_of(j * 32, 32), 32)
        vals = []
        for b in range(8):
            lanes = slice((b % 2) * 128, (b % 2) * 128 + 128)
            v = u[b : b + 1, :] + sc[b // 2, rows, lanes]
            sc[b // 2, rows, lanes] = v
            vals.append(v)
        peak = vals[0]
        for v in vals[1:]:
            peak = jnp.maximum(peak, v)
        total = jnp.exp2(vals[0] - peak)
        for v in vals[1:]:
            total = total + jnp.exp2(v - peak)
        cl[rows, :] = peak + LOG2E * jnp.log(total)
        return carry

    lax.fori_loop(0, 16, columns, 0, unroll=True)
    tops = []
    for b in range(4):
        turned = cl[b * 128 : (b + 1) * 128, :].T
        tops.append(jnp.max(turned, axis=0, keepdims=True))
        cb[pl.ds(me, 1), b : b + 1] = lse0(turned)[None]

    pl.semaphore_wait(known, 4)

    def send_columns(d, to_c):
        remote(cb.at[me], cb.at[me], cb_s.at[0], cb_r.at[0], column_device((z + d) & 15, to_c)).start()

    for d in (8, 7, -7, 6, -6, 5, -5, 4, -4, 3, -3, 2, -2, 1, -1):
        for to_c in range(2):
            send_columns(d, to_c)
    send_columns(0, 1 - c)

    own_lse = uu[pl.ds(q >> 1, 1), :]
    own_lse = jnp.where(q & 1 == 0, own_lse, pltpu.roll(own_lse, 64, 1))
    out_f[...] = 0.5 * (lsv[...] + norm[:, 0:ROWS] - LN2 * own_lse[:, 0:ROWS])

    def weights(j, carry):
        rows = pl.ds(pl.multiple_of(j * 32, 32), 32)
        top = jnp.max(cl[rows, :], axis=1, keepdims=True)
        for quad in range(4):
            w = jnp.exp2(sc[quad, rows, :] - top)
            hi = w.astype(BF16)
            eh[quad, rows, :] = hi
            el[quad, rows, :] = (w - hi.astype(F32)).astype(BF16)
        return carry

    lax.fori_loop(0, 16, weights, 0)

    take(cb.at[pl.ds(0, 31)], cb_r.at[0])
    collse = lse0(cb[...])[0]
    mp[...] = collse
    new_row = mp[pl.ds(t >> 2, 1), :]
    factor = jnp.exp2(log_target + jnp.concatenate(tops, axis=0) - collse)
    lead = lax.broadcasted_iota(jnp.int32, (16, 128), 0)
    for b in range(4):
        lanes = slice(b * 128, (b + 1) * 128)
        f = factor[b : b + 1, :]
        scaled = yt[:, lanes] * f
        hi = scaled.astype(BF16)
        fs[0:128, lanes] = hi
        fs[144:272, lanes] = (scaled - hi.astype(F32)).astype(BF16)
        top = f.astype(BF16).astype(F32)
        fs[128:144, lanes] = jnp.where(lead == 0, top, jnp.where(lead == 1, f - top, 0.0)).astype(BF16)

    for a in (2, 1, 3, 0):
        quad = (x + a) & 3
        first = jnp.dot(fs[...], eh[pl.ds(quad, 1)][0], preferred_element_type=F32)
        second = jnp.dot(fs[0:144, :], el[pl.ds(quad, 1)][0], preferred_element_type=F32)
        n = first[0:128] + first[144:272] + second[0:128]
        total = first[128:129] + first[129:130] + second[128:129]
        n = jnp.concatenate([n[:, 0:128].T, n[:, 128:256].T], axis=0)
        for h in range(4):
            lanes = slice((h // 2) * 128, (h // 2) * 128 + 128)
            part = jnp.concatenate([n[h * ROWS : (h + 1) * ROWS], total[:, lanes], new_row], axis=0)
            mm[pl.ds(quad * 4 + h, 1)] = part[None]
    for a in (2, 1, 3, 0):
        for b in (2, 1, 3, 0):
            if a or b:
                p = peer(a, b)
                remote(mm.at[p], mb.at[q], mb_s.at[0], mb_r.at[x], plane_device(p)).start()

    mb[pl.ds(q, 1)] = mm[pl.ds(q, 1)]
    total = jnp.zeros((ROWS + 1, 128), F32)
    for a in range(4):
        take(mb.at[pl.ds(0, 4 if a else 3)], mb_r.at[(x + a) & 3])
    for quad in range(4):
        got = mb[pl.ds(quad * 4, 4), 0 : ROWS + 1]
        total = total + ((got[0] + got[1]) + (got[2] + got[3]))
    wt[...] = jnp.broadcast_to(1.0 / total[ROWS : ROWS + 1], (128, 128)).T
    out_m[...] = total[0:ROWS] * wt[pl.ds(pl.multiple_of((q & 1) * ROWS, ROWS), ROWS), :]

    new = gather_lanes(mb[:, ROWS + 1 : ROWS + 2].reshape(16, 128), t & 3)
    out_t[...] = gv[...] + 0.5 * (lv[...] - LN2 * new)

    left(tb.at[pl.ds(0, 15)], tb_s.at[0])
    left(xs.at[pl.ds(0, 15)], xs_s.at[0])
    left(rb.at[pl.ds(0, 15)], rb_s.at[0])
    left(cb.at[pl.ds(0, 31)], cb_s.at[0])
    left(mm.at[pl.ds(0, 15)], mb_s.at[0])


def finish(f_ref, t_ref, m_ref, out_f, out_t, out_m):
    out_f[...] = f_ref[...]
    out_t[...] = t_ref[...]
    out_m[...] = m_ref[...]


def shards(points_src, points_tgt, log_source, log_target, target_potential):
    vmem = pl.BlockSpec(memory_space=pltpu.VMEM)
    hbm = pl.BlockSpec(memory_space=pltpu.HBM)
    dma = pltpu.SemaphoreType.DMA
    shapes = (
        jax.ShapeDtypeStruct((1, ROWS), F32),
        jax.ShapeDtypeStruct((4, 128), F32),
        jax.ShapeDtypeStruct((ROWS, 128), F32),
    )
    results = pl.pallas_call(
        kernel,
        name="sinkhorn",
        out_shape=tuple(pltpu.VMEM(v.shape, v.dtype) for v in shapes),
        in_specs=[hbm] * 5,
        out_specs=(vmem,) * 3,
        scratch_shapes=[
            pltpu.VMEM((16, ROWS, 128), F32),
            pltpu.VMEM((16, SLICE + 2, 128), F32),
            pltpu.VMEM((4, 128), F32),
            pltpu.VMEM((4, 128), F32),
            pltpu.VMEM((1, ROWS), F32),
            pltpu.VMEM((512, 256), BF16),
            pltpu.VMEM((512, 256), BF16),
            pltpu.VMEM((512, 128), F32),
            pltpu.VMEM((128, 512), F32),
            pltpu.VMEM((512, 128), F32),
            pltpu.VMEM((4, 512, QUAD), F32),
            pltpu.VMEM((4, 512, QUAD), BF16),
            pltpu.VMEM((4, 512, QUAD), BF16),
            pltpu.VMEM((272, 512), BF16),
            pltpu.VMEM((16, 9, 128), F32),
            pltpu.VMEM((8, 128), F32),
            pltpu.VMEM((8, 128), F32),
            pltpu.VMEM((512, 128), F32),
            pltpu.VMEM((32, 4, 128), F32),
            pltpu.VMEM((4, 128), F32),
            pltpu.VMEM((16, ROWS + 2, 128), F32),
            pltpu.VMEM((16, ROWS + 2, 128), F32),
            pltpu.VMEM((128, 128), F32),
            pltpu.SemaphoreType.REGULAR,
            dma((5,)),
            dma((1,)), dma((7,)),
            dma((1,)), dma((5,)), dma((3,)),
            dma((1,)), dma((1,)),
            dma((1,)), dma((1,)),
            dma((1,)), dma((4,)),
        ],
        compiler_params=pltpu.CompilerParams(
            collective_id=0, has_side_effects=True, vmem_limit_bytes=40 * 2**20
        ),
    )(
        *(
            pltpu.with_memory_space_constraint(v, pltpu.HBM)
            for v in (
                points_src,
                points_tgt,
                log_source.reshape(1, ROWS),
                log_target.reshape(4, 128),
                target_potential.reshape(4, 128),
            )
        )
    )
    source_potential, target_new, mapped = pl.pallas_call(
        finish, name="finish", out_shape=shapes, in_specs=[vmem] * 3, out_specs=(vmem,) * 3
    )(*(pltpu.with_memory_space_constraint(v, pltpu.VMEM) for v in results))
    return source_potential.reshape(ROWS), target_new.reshape(512), mapped


def solution(mesh):
    return jax.shard_map(
        shards,
        mesh=mesh,
        in_specs=(P(("src", "tgt"), None), P("tgt", None), P(("src", "tgt")), P("tgt"), P("tgt")),
        out_specs=(P(("src", "tgt")), P("tgt"), P(("src", "tgt"), None)),
        check_vma=False,
    )
```

```python
import jax
import jax.numpy as jnp
from jax import lax
from jax.experimental import pallas as pl
from jax.experimental.pallas import tpu as pltpu
from jax.sharding import PartitionSpec as P

MESH = pl.DeviceIdType.MESH
F32 = jnp.float32
BF16 = jnp.bfloat16
ROWS = 64
HALF = 32
SLICE = 32
QUAD = 4 * ROWS


def ring(a):
    return min(a, 4 - a)


PEERS = sorted(((a, b) for a in range(4) for b in range(4) if a or b), key=lambda o: -ring(o[0]) - ring(o[1]))

LOG2E = 1.4426950408889634
LN2 = 0.6931471805599453


def lse0(values):
    peak = jnp.max(values, axis=0, keepdims=True)
    return peak + LOG2E * jnp.log(jnp.sum(jnp.exp2(values - peak), axis=0, keepdims=True))


def split3(v):
    hi = v.astype(BF16)
    rest = v - hi.astype(F32)
    mid = rest.astype(BF16)
    return hi, mid, (rest - mid.astype(F32)).astype(BF16)


def gather_lanes(pieces, group):
    lane = lax.broadcasted_iota(jnp.int32, (16, 128), 1) >> 5
    row = lax.broadcasted_iota(jnp.int32, (16, 128), 0) & 3
    whole = jnp.zeros((16, 128), F32)
    for k in range(4):
        turned = pltpu.roll(pieces, ((k - group) & 3) * SLICE, 1)
        whole = whole + jnp.where((lane == k) & (row == k), turned, 0.0)
    return jnp.concatenate([jnp.sum(whole[4 * b : 4 * b + 4], axis=0, keepdims=True) for b in range(4)], axis=0)


def kernel(
    ps, pt, ls, lt, gp,
    out_f, out_t, out_m,
    xs, tb, gv, lv, lsv, y1, y3, yf, yt, aa, sc, eh, el, fs, rb, uu, lsum, cl, cb, mp, mm, mb, wt,
    known, loc, xs_s, xs_r, tb_s, tb_r, fw_r, rb_s, rb_r, cb_s, cb_r, mb_s, mb_r,
):
    s = lax.axis_index("src")
    t = lax.axis_index("tgt")
    q = s >> 1
    zl = t >> 1
    c = t & 1
    z = (s & 1) * 8 + zl
    x = q >> 2
    y = q & 3
    me = z * 2 + c

    def peer(a, b):
        return ((x + a) & 3) * 4 + ((y + b) & 3)

    def plane_device(p):
        return (p * 2 + (s & 1), t)

    def column_device(to_z, to_c):
        return (q * 2 + (to_z >> 3), (to_z & 7) * 2 + to_c)

    def remote(src, dst, send, recv, device):
        return pltpu.make_async_remote_copy(
            src_ref=src, dst_ref=dst, send_sem=send, recv_sem=recv, device_id=device, device_id_type=MESH
        )

    def take(ref, recv):
        remote(ref, ref, recv, recv, plane_device(peer(1, 0))).wait_recv()

    def left(ref, send):
        remote(ref, ref, send, send, plane_device(peer(1, 0))).wait_send()

    barrier = pltpu.get_barrier_semaphore()

    def greet(device, sem=barrier):
        pl.semaphore_signal(sem, inc=1, device_id=device, device_id_type=MESH)

    sibling = column_device(z, 1 - c)
    for k in (2, 1, 3):
        greet(plane_device(peer(k, 0)))
        greet(plane_device(peer(0, k)))
    for d in (2, -2, 1, -1):
        greet(column_device((z + d) & 15, c))
    greet(sibling)

    local = [
        pltpu.make_async_copy(gp, gv, loc.at[0]),
        pltpu.make_async_copy(lt, lv, loc.at[1]),
        pltpu.make_async_copy(pt.at[pl.ds(pl.multiple_of(q * SLICE, SLICE), SLICE)], tb.at[t, pl.ds(0, SLICE)], loc.at[2]),
        pltpu.make_async_copy(ps, xs.at[q], loc.at[3]),
        pltpu.make_async_copy(ls, lsv, loc.at[4]),
    ]
    for copy in local:
        copy.start()
    for copy in local:
        copy.wait()
    tb[pl.ds(t, 1), SLICE : SLICE + 1] = gv[pl.ds(q >> 2, 1), :][None]
    tb[pl.ds(t, 1), SLICE + 1 : SLICE + 2] = lv[pl.ds(q >> 2, 1), :][None]

    pl.semaphore_wait(barrier, 6 + 4 + 1)

    def send_targets(slot, recv, device):
        remote(tb.at[slot], tb.at[slot], tb_s.at[0], recv, device).start()

    def send_half(p, h, recv, to):
        part = xs.at[p, pl.ds(h * HALF, HALF)]
        remote(part, part, xs_s.at[0], recv, plane_device(to)).start()

    def pass_on(p, h):
        for k in (2, 1, 3):
            send_half(p, h, xs_r.at[0], peer(k, 0) if h else peer(0, k))

    def column_slot(off, core):
        return ((zl + off) & 7) * 2 + core

    send_targets(t, tb_r.at[1], column_device((z + 2) & 15, c))
    send_targets(t, tb_r.at[2], column_device((z - 2) & 15, c))
    for k in (1, 3, 2):
        send_half(q, 0, xs_r.at[k], peer(k, 0))
        send_half(q, 1, xs_r.at[3 + k], peer(0, k))
    for d in (1, -1):
        send_targets(t, tb_r.at[0], column_device((z + d) & 15, c))
    pass_on(q, 0)
    pass_on(q, 1)
    send_targets(t, fw_r.at[0], sibling)
    half_block = xs.at[0, pl.ds(0, HALF)]

    def relay_points(k):
        take(half_block, xs_r.at[k])
        pass_on(peer(-k, 0), 0)
        take(half_block, xs_r.at[3 + k])
        pass_on(peer(0, -k), 1)

    relay_points(1)
    take(tb.at[pl.ds(0, 2)], tb_r.at[0])
    take(tb.at[0], tb_r.at[1])
    take(tb.at[0], tb_r.at[2])
    turn = 2 - 4 * c
    for core in range(2):
        send_targets(column_slot(-turn, c), tb_r.at[4], column_device((z + turn) & 15, core))
    for sign in (1, -1):
        for core in range(2):
            send_targets(column_slot(-2 * sign, c), tb_r.at[3], column_device((z + sign) & 15, core))
    relay_points(3)
    relay_points(2)
    for d in (1, 2):
        for off in (d, 8 - d):
            send_targets(column_slot(off, c), fw_r.at[d], sibling)

    lane = lax.broadcasted_iota(jnp.int32, (SLICE, 128), 1)
    sub = lax.broadcasted_iota(jnp.int32, (SLICE, 128), 0)
    mine = lane == sub + (q & 3) * SLICE

    def use_targets(slot):
        block = tb[pl.ds(slot, 1)][0]
        pts = block[0:SLICE]
        rows = pl.ds(pl.multiple_of(slot * SLICE, SLICE), SLICE)
        own = jnp.where(mine, 2.0 * block[SLICE : SLICE + 1], 0.0)
        a = LOG2E * jnp.sum(own - pts * pts, axis=1, keepdims=True)
        aa[rows, :] = jnp.broadcast_to(a, (SLICE, 128))
        hi, mid, lo = split3((2.0 * LOG2E) * pts)
        yf[rows, :] = pts
        y1[rows, 0:128] = hi
        y1[rows, 128:256] = mid
        y3[rows, 0:128] = hi
        y3[rows, 128:256] = lo

    groups = (
        (fw_r.at[0], 1, (0,)),
        (fw_r.at[1], 2, (1, 7)),
        (fw_r.at[2], 2, (2, 6)),
        (tb_r.at[4], 2, (4,)),
        (tb_r.at[3], 4, (3, 5)),
    )
    for sem, count, offsets in groups:
        take(tb.at[pl.ds(0, count)], sem)
        for off in offsets:
            for core in range(2):
                use_targets(column_slot(off, core))
    for d in (2, -2):
        for core in range(2):
            greet(column_device((z + d) & 15, core), known)

    def product(targets, first, second):
        return lax.dot_general(
            targets, jnp.concatenate([first, second], axis=1),
            (((1,), (1,)), ((), ())), preferred_element_type=F32,
        )

    take(xs.at[pl.ds(0, 12)], xs_r.at[0])
    for quad in range(4):
        hi, mid, lo = split3(xs[quad * 4 : quad * 4 + 4].reshape(QUAD, 128))
        prod = product(y3[...], lo, hi) + product(y1[...], mid, hi) + product(y1[...], hi, mid)
        score = prod + jnp.concatenate([aa[...], aa[...]], axis=1)
        sc[quad] = score
        row = lse0(score)
        rb[pl.ds(q, 1), 2 * quad : 2 * quad + 1] = row[:, 0:128][None]
        rb[pl.ds(q, 1), 2 * quad + 1 : 2 * quad + 2] = row[:, 128:256][None]

    half = (lax.broadcasted_iota(jnp.int32, (1, 128), 1) >> 6) == (q & 1)
    both = jnp.concatenate([lsv[...], lsv[...]], axis=1)
    rb[pl.ds(q, 1), 8:9] = jnp.where(half, both, 0.0)[None]
    for a, b in PEERS:
        remote(rb.at[q], rb.at[q], rb_s.at[0], rb_r.at[0], plane_device(peer(a, b))).start()

    for b in range(4):
        yt[:, b * 128 : (b + 1) * 128] = yf[b * 128 : (b + 1) * 128, :].T
    log_target = LOG2E * gather_lanes(tb[:, SLICE + 1 : SLICE + 2].reshape(16, 128), q & 3)
    own_points = xs[pl.ds(q, 1)][0]
    squares = jnp.concatenate([own_points * own_points, jnp.zeros((128 - ROWS, 128), F32)], axis=0)
    norm = jnp.sum(squares.T, axis=0, keepdims=True)

    take(rb.at[pl.ds(0, 15)], rb_r.at[0])
    rowlse = lse0(rb[:, 0:8])[0]
    uu[...] = rowlse
    for b in range(8):
        lsum[b : b + 1, :] = rb[2 * b, 8:9] + rb[2 * b + 1, 8:9]
    u = LOG2E * lsum[...] - rowlse

    def columns(j, carry):
        rows = pl.ds(pl.multiple_of(j * 32, 32), 32)
        vals = []
        for b in range(8):
            lanes = slice((b % 2) * 128, (b % 2) * 128 + 128)
            v = u[b : b + 1, :] + sc[b // 2, rows, lanes]
            sc[b // 2, rows, lanes] = v
            vals.append(v)
        peak = vals[0]
        for v in vals[1:]:
            peak = jnp.maximum(peak, v)
        total = jnp.exp2(vals[0] - peak)
        for v in vals[1:]:
            total = total + jnp.exp2(v - peak)
        cl[rows, :] = peak + LOG2E * jnp.log(total)
        return carry

    lax.fori_loop(0, 16, columns, 0, unroll=True)
    tops = []
    for b in range(4):
        turned = cl[b * 128 : (b + 1) * 128, :].T
        tops.append(jnp.max(turned, axis=0, keepdims=True))
        cb[pl.ds(me, 1), b : b + 1] = lse0(turned)[None]

    pl.semaphore_wait(known, 4)

    def send_columns(d, to_c):
        remote(cb.at[me], cb.at[me], cb_s.at[0], cb_r.at[0], column_device((z + d) & 15, to_c)).start()

    for d in (8, 7, -7, 6, -6, 5, -5, 4, -4, 3, -3, 2, -2, 1, -1):
        for to_c in range(2):
            send_columns(d, to_c)
    send_columns(0, 1 - c)

    own_lse = uu[pl.ds(q >> 1, 1), :]
    own_lse = jnp.where(q & 1 == 0, own_lse, pltpu.roll(own_lse, 64, 1))
    out_f[...] = 0.5 * (lsv[...] + norm[:, 0:ROWS] - LN2 * own_lse[:, 0:ROWS])

    def weights(j, carry):
        rows = pl.ds(pl.multiple_of(j * 32, 32), 32)
        top = jnp.max(cl[rows, :], axis=1, keepdims=True)
        for quad in range(4):
            w = jnp.exp2(sc[quad, rows, :] - top)
            hi = w.astype(BF16)
            eh[quad, rows, :] = hi
            el[quad, rows, :] = (w - hi.astype(F32)).astype(BF16)
        return carry

    lax.fori_loop(0, 16, weights, 0)

    take(cb.at[pl.ds(0, 31)], cb_r.at[0])
    collse = lse0(cb[...])[0]
    mp[...] = collse
    new_row = mp[pl.ds(t >> 2, 1), :]
    factor = jnp.exp2(log_target + jnp.concatenate(tops, axis=0) - collse)
    lead = lax.broadcasted_iota(jnp.int32, (16, 128), 0)
    for b in range(4):
        lanes = slice(b * 128, (b + 1) * 128)
        f = factor[b : b + 1, :]
        scaled = yt[:, lanes] * f
        hi = scaled.astype(BF16)
        fs[0:128, lanes] = hi
        fs[144:272, lanes] = (scaled - hi.astype(F32)).astype(BF16)
        top = f.astype(BF16).astype(F32)
        fs[128:144, lanes] = jnp.where(lead == 0, top, jnp.where(lead == 1, f - top, 0.0)).astype(BF16)

    for a in (2, 1, 3, 0):
        quad = (x + a) & 3
        first = jnp.dot(fs[...], eh[pl.ds(quad, 1)][0], preferred_element_type=F32)
        second = jnp.dot(fs[0:144, :], el[pl.ds(quad, 1)][0], preferred_element_type=F32)
        n = first[0:128] + first[144:272] + second[0:128]
        total = first[128:129] + first[129:130] + second[128:129]
        n = jnp.concatenate([n[:, 0:128].T, n[:, 128:256].T], axis=0)
        for h in range(4):
            lanes = slice((h // 2) * 128, (h // 2) * 128 + 128)
            part = jnp.concatenate([n[h * ROWS : (h + 1) * ROWS], total[:, lanes], new_row], axis=0)
            mm[pl.ds(quad * 4 + h, 1)] = part[None]
    for a in (2, 1, 3, 0):
        for b in (2, 1, 3, 0):
            if a or b:
                p = peer(a, b)
                remote(mm.at[p], mb.at[q], mb_s.at[0], mb_r.at[0], plane_device(p)).start()

    mb[pl.ds(q, 1)] = mm[pl.ds(q, 1)]
    total = jnp.zeros((ROWS + 1, 128), F32)
    take(mb.at[pl.ds(0, 15)], mb_r.at[0])
    for quad in range(4):
        got = mb[pl.ds(quad * 4, 4), 0 : ROWS + 1]
        total = total + ((got[0] + got[1]) + (got[2] + got[3]))
    wt[...] = jnp.broadcast_to(1.0 / total[ROWS : ROWS + 1], (128, 128)).T
    out_m[...] = total[0:ROWS] * wt[pl.ds(pl.multiple_of((q & 1) * ROWS, ROWS), ROWS), :]

    new = gather_lanes(mb[:, ROWS + 1 : ROWS + 2].reshape(16, 128), t & 3)
    out_t[...] = gv[...] + 0.5 * (lv[...] - LN2 * new)

    left(tb.at[pl.ds(0, 15)], tb_s.at[0])
    left(xs.at[pl.ds(0, 15)], xs_s.at[0])
    left(rb.at[pl.ds(0, 15)], rb_s.at[0])
    left(cb.at[pl.ds(0, 31)], cb_s.at[0])
    left(mm.at[pl.ds(0, 15)], mb_s.at[0])


def finish(f_ref, t_ref, m_ref, out_f, out_t, out_m):
    out_f[...] = f_ref[...]
    out_t[...] = t_ref[...]
    out_m[...] = m_ref[...]


def shards(points_src, points_tgt, log_source, log_target, target_potential):
    vmem = pl.BlockSpec(memory_space=pltpu.VMEM)
    hbm = pl.BlockSpec(memory_space=pltpu.HBM)
    dma = pltpu.SemaphoreType.DMA
    shapes = (
        jax.ShapeDtypeStruct((1, ROWS), F32),
        jax.ShapeDtypeStruct((4, 128), F32),
        jax.ShapeDtypeStruct((ROWS, 128), F32),
    )
    results = pl.pallas_call(
        kernel,
        name="sinkhorn",
        out_shape=tuple(pltpu.VMEM(v.shape, v.dtype) for v in shapes),
        in_specs=[hbm] * 5,
        out_specs=(vmem,) * 3,
        scratch_shapes=[
            pltpu.VMEM((16, ROWS, 128), F32),
            pltpu.VMEM((16, SLICE + 2, 128), F32),
            pltpu.VMEM((4, 128), F32),
            pltpu.VMEM((4, 128), F32),
            pltpu.VMEM((1, ROWS), F32),
            pltpu.VMEM((512, 256), BF16),
            pltpu.VMEM((512, 256), BF16),
            pltpu.VMEM((512, 128), F32),
            pltpu.VMEM((128, 512), F32),
            pltpu.VMEM((512, 128), F32),
            pltpu.VMEM((4, 512, QUAD), F32),
            pltpu.VMEM((4, 512, QUAD), BF16),
            pltpu.VMEM((4, 512, QUAD), BF16),
            pltpu.VMEM((272, 512), BF16),
            pltpu.VMEM((16, 9, 128), F32),
            pltpu.VMEM((8, 128), F32),
            pltpu.VMEM((8, 128), F32),
            pltpu.VMEM((512, 128), F32),
            pltpu.VMEM((32, 4, 128), F32),
            pltpu.VMEM((4, 128), F32),
            pltpu.VMEM((16, ROWS + 2, 128), F32),
            pltpu.VMEM((16, ROWS + 2, 128), F32),
            pltpu.VMEM((128, 128), F32),
            pltpu.SemaphoreType.REGULAR,
            dma((5,)),
            dma((1,)), dma((7,)),
            dma((1,)), dma((5,)), dma((3,)),
            dma((1,)), dma((1,)),
            dma((1,)), dma((1,)),
            dma((1,)), dma((1,)),
        ],
        compiler_params=pltpu.CompilerParams(
            collective_id=0, has_side_effects=True, vmem_limit_bytes=40 * 2**20
        ),
    )(
        *(
            pltpu.with_memory_space_constraint(v, pltpu.HBM)
            for v in (
                points_src,
                points_tgt,
                log_source.reshape(1, ROWS),
                log_target.reshape(4, 128),
                target_potential.reshape(4, 128),
            )
        )
    )
    source_potential, target_new, mapped = pl.pallas_call(
        finish, name="finish", out_shape=shapes, in_specs=[vmem] * 3, out_specs=(vmem,) * 3
    )(*(pltpu.with_memory_space_constraint(v, pltpu.VMEM) for v in results))
    return source_potential.reshape(ROWS), target_new.reshape(512), mapped


def solution(mesh):
    return jax.shard_map(
        shards,
        mesh=mesh,
        in_specs=(P(("src", "tgt"), None), P("tgt", None), P(("src", "tgt")), P("tgt"), P("tgt")),
        out_specs=(P(("src", "tgt")), P("tgt"), P(("src", "tgt"), None)),
        check_vma=False,
    )
```
